128 devices in a mesh: rows: 4 (over x_lo, core), cols: 32 (over y, x_hi, z).
Axes of the slice: x: 4 (x_hi: 2, x_lo: 2; x = x_hi * 2 + x_lo), y: 4, z: 4, core: 2. Of those that a mesh axis runs over, the one named last changes fastest.
Arguments:
- image: bfloat16 [128, 2048, 128], P('rows', 'cols'), may hold values from -40 to 40
- cotangent: bfloat16 [128, 2048, 128], P('rows', 'cols'), may hold values from -6 to 6
- norm1_gain: float32 [128], replicated, may hold values from 0.1 to 1.9
- w_expand: float32 [128, 512], replicated, may hold values from -0.5 to 0.5
- dw_kernel: float32 [9, 512], replicated, may hold values from -2 to 2
- w_project: float32 [512, 128], replicated, may hold values from -0.25 to 0.25
- norm2_gain: float32 [128], replicated, may hold values from 0.1 to 1.9
- w_qkv: float32 [128, 384], replicated, may hold values from -0.5 to 0.5
- w_out: float32 [128, 128], replicated, may hold values from -0.5 to 0.5
- bias_table: float32 [4, 225], replicated, may hold values from -80 to 160
Outputs:
- block_out: bfloat16 [128, 2048, 128], P('rows', 'cols')
- grad_image: bfloat16 [128, 2048, 128], P('rows', 'cols')
- grad_gain1: float32 [128], replicated
- grad_expand: float32 [128, 512], replicated
- grad_kernel: float32 [9, 512], replicated
- grad_project: float32 [512, 128], replicated
- grad_gain2: float32 [128], replicated
- grad_qkv: float32 [128, 384], replicated
- grad_out: float32 [128, 128], replicated
- grad_bias: float32 [4, 225], replicated
The draws below stay inside these ranges and needn't reach their ends.
All inputs are finite; a program needn't handle non-finite values.
Results may differ from the reference program's by a relative error of at most 0.019.
Values may be sent and summed in bfloat16 or wider, within the bound.
No kernel may reach another device: no remote copies, remote signals or barrier semaphores. Data moves between devices by JAX's collectives and lax.ppermute only.
A program may use at most 128 MiB of HBM per device.

```python
import math
import jax
import jax.numpy as jnp
from jax import lax

C = 128
E = 512
HEADS = 4
GRID = 8
RD = 32
TABLE = 225
HH = 128
WW = 2048
TOKENS = 262144


def draw_image(key, part):
    key = jax.random.fold_in(key, 3)
    key_base, key_chan, key_spot = jax.random.split(key, 3)
    channel_scale = jnp.exp(jax.random.uniform(key_chan, (1, 1, C), jnp.float32, 0.0, math.log(10.0)))
    token_scale = jnp.exp(jax.random.uniform(key_spot, (HH, WW, 1), jnp.float32, 0.0, math.log(10.0)))
    base_draw = jnp.clip(jax.random.normal(key_base, (HH, WW, C), jnp.float32), -4.0, 4.0)
    return (0.1 * base_draw * channel_scale * token_scale).astype(jnp.bfloat16)


def draw_bias_table(key, part):
    key = jax.random.fold_in(key, 5)
    key_base = jax.random.fold_in(key, 0)
    return jnp.clip(jax.random.normal(key_base, (HEADS, TABLE), jnp.float32), -4.0, 4.0)


def steps_of(rng, extent, cuts, low, high):
    level = 1.0
    for position, blocks in cuts:
        heights = jax.random.uniform(jax.random.fold_in(jax.random.fold_in(rng, 6), position), (blocks,), jnp.float32, low / len(cuts), high / len(cuts))
        level = level * jnp.repeat(jnp.exp(heights), extent[position] // blocks).reshape((-1,) + (1,) * (len(extent) - 1 - position))
    return level


def bell_draw(own_key, dims, scale, bound, cuts=(), held_as=jnp.bfloat16):
    result = scale * jax.random.normal(own_key, dims, jnp.float32)
    if cuts:
        result = result * steps_of(own_key, dims, cuts, -0.22, 0.18)
    return jnp.clip(result, -bound, bound).astype(held_as)


def setup_inputs(seed: int = 0) -> dict:
    key_list = jax.random.split(jax.random.key(seed), 11)
    image = draw_image(jax.random.fold_in(key_list[10], 71), 0)
    cotangent = bell_draw(key_list[1], (HH, WW, C), 1.0, 6.0, ((0, 4), (1, 32)))
    norm1_gain = jnp.clip(1.0 + 0.18 * jax.random.normal(key_list[2], (C,), jnp.float32), 0.1, 1.9)
    w_expand = bell_draw(key_list[3], (C, E), C ** -0.5, 0.5, (), jnp.float32)
    dw_kernel = bell_draw(key_list[4], (9, E), 9 ** -0.5, 2.0, (), jnp.float32)
    w_project = bell_draw(key_list[5], (E, C), E ** -0.5, 0.25, (), jnp.float32)
    norm2_gain = jnp.clip(1.0 + 0.18 * jax.random.normal(key_list[6], (C,), jnp.float32), 0.1, 1.9)
    w_qkv = bell_draw(key_list[7], (C, 3 * C), C ** -0.5, 0.5, (), jnp.float32)
    w_out = bell_draw(key_list[8], (C, C), C ** -0.5, 0.5, (), jnp.float32)
    bias_table = draw_bias_table(jax.random.fold_in(key_list[10], 71), 0)
    return dict(image=image, cotangent=cotangent, norm1_gain=norm1_gain, w_expand=w_expand, dw_kernel=dw_kernel, w_project=w_project, norm2_gain=norm2_gain, w_qkv=w_qkv, w_out=w_out, bias_table=bias_table)


epsilon = 1e-06
gelu_coef = math.sqrt(2.0 / math.pi)

def gelu_value(values):
    inner = gelu_coef * (values + 0.044715 * values * values * values)
    return 0.5 * values * (1.0 + jnp.tanh(inner))

def gelu_slope(values):
    tangent = jnp.tanh(gelu_coef * (values + 0.044715 * values * values * values))
    return 0.5 * (1.0 + tangent) + 0.5 * values * (1.0 - tangent * tangent) * gelu_coef * (1.0 + 0.134145 * values * values)

def expand_part(tokens, gain_vec, weight):
    values = tokens.astype(jnp.float32)
    inverse = lax.rsqrt(lax.optimization_barrier(jnp.mean(values * values, axis=-1, keepdims=True)) + epsilon)
    unit_form = values * inverse
    normed = (unit_form * gain_vec).astype(jnp.bfloat16)
    flat_rows = normed.reshape(-1, normed.shape[-1])
    before = jnp.dot(flat_rows, weight, preferred_element_type=jnp.float32)
    before = before.reshape(normed.shape[:-1] + (weight.shape[1],))
    return (inverse, unit_form, normed, before, gelu_value(before).astype(jnp.bfloat16))

def depthwise(padded, kernel, height, breadth):
    running = jnp.zeros((height, breadth, kernel.shape[1]), jnp.float32)
    for offset in range(9):
        window = padded[offset // 3:offset // 3 + height, offset % 3:offset % 3 + breadth]
        running = running + kernel[offset] * window.astype(jnp.float32)
    return running

def offsets_onehot():
    member_count = GRID * GRID
    span_size = 2 * GRID - 1
    pair_index = jnp.arange(member_count * member_count, dtype=jnp.int32)
    first_pos = pair_index // member_count
    second_pos = pair_index % member_count
    table_index = (first_pos // GRID - second_pos // GRID + GRID - 1) * span_size + (first_pos % GRID - second_pos % GRID + GRID - 1)
    return (table_index[:, None] == jnp.arange(span_size * span_size, dtype=jnp.int32)[None, :]).astype(jnp.float32)

def attend_forward(windows, weight, bias_full, head_count):
    window_count, member_count, channels = windows.shape
    head_size = channels // head_count
    mixture = jnp.dot(windows.reshape(-1, channels), weight, preferred_element_type=jnp.float32)
    mixture = mixture.reshape(window_count, member_count, 3, head_count, head_size)
    queries = (mixture[:, :, 0] * head_size ** (-0.5)).astype(jnp.bfloat16)
    key_vecs = mixture[:, :, 1].astype(jnp.bfloat16)
    value_vecs = mixture[:, :, 2].astype(jnp.bfloat16)
    scores = jnp.einsum('wihd,wjhd->whij', queries.astype(jnp.float32), key_vecs.astype(jnp.float32)) + bias_full[None]
    row_max = lax.optimization_barrier(jnp.max(scores, axis=-1, keepdims=True))
    weights = jnp.exp(scores - row_max)
    probability = weights / lax.optimization_barrier(jnp.sum(weights, axis=-1, keepdims=True))
    rounded = probability.astype(jnp.bfloat16)
    attended = jnp.einsum('whij,wjhd->wihd', rounded.astype(jnp.float32), value_vecs.astype(jnp.float32))
    attended = attended.astype(jnp.bfloat16).reshape(window_count, member_count, channels)
    return (attended, queries, key_vecs, value_vecs, probability, rounded)

def attend_backward(windows, grad_attended, weight, queries, key_vecs, value_vecs, probability, rounded, head_count):
    window_count, member_count, channels = windows.shape
    head_size = channels // head_count
    grad_heads = grad_attended.reshape(window_count, member_count, head_count, head_size).astype(jnp.float32)
    grad_probs = jnp.einsum('wihd,wjhd->whij', grad_heads, value_vecs.astype(jnp.float32))
    grad_values = jnp.einsum('whij,wihd->wjhd', rounded.astype(jnp.float32), grad_heads)
    grad_scores = probability * (grad_probs - lax.optimization_barrier(jnp.sum(probability * grad_probs, axis=-1, keepdims=True)))
    grad_round = grad_scores.astype(jnp.bfloat16).astype(jnp.float32)
    grad_queries = jnp.einsum('whij,wjhd->wihd', grad_round, key_vecs.astype(jnp.float32))
    grad_keys = jnp.einsum('whij,wihd->wjhd', grad_round, queries.astype(jnp.float32))
    grad_mixture = jnp.stack([grad_queries * head_size ** (-0.5), grad_keys, grad_values], axis=2)
    grad_mixture = grad_mixture.astype(jnp.bfloat16).reshape(-1, 3 * channels)
    grad_weight = jnp.dot(windows.reshape(-1, channels).T, grad_mixture, preferred_element_type=jnp.float32)
    grad_windows = jnp.dot(grad_mixture, weight.T, preferred_element_type=jnp.float32)
    grad_windows = grad_windows.astype(jnp.bfloat16).reshape(window_count, member_count, channels)
    return (grad_windows, grad_weight, lax.optimization_barrier(jnp.sum(grad_scores, axis=0)))

def reference(image, cotangent, norm1_gain, w_expand, dw_kernel, w_project, norm2_gain, w_qkv, w_out, bias_table):
    expand_half = w_expand.astype(jnp.bfloat16)
    project_half = w_project.astype(jnp.bfloat16)
    mixing_half = w_qkv.astype(jnp.bfloat16)
    output_half = w_out.astype(jnp.bfloat16)
    factor = 1.0 / math.sqrt(TOKENS)
    onehot = offsets_onehot()
    bias_full = jnp.dot(bias_table, onehot.T, precision=lax.Precision.HIGHEST).reshape(HEADS, GRID * GRID, GRID * GRID)
    strips = HH // RD
    strip_ids = jnp.arange(strips, dtype=jnp.int32)
    padded_image = jnp.pad(image, ((2, 2), (0, 0), (0, 0)))

    def forward_strip(strip_index):
        first_row = (strip_index * RD + 1).astype(jnp.int32)
        rows_in = lax.dynamic_slice_in_dim(padded_image, first_row, RD + 2, 0)
        expanded = expand_part(rows_in, norm1_gain, expand_half)[4]
        expand_rim = jnp.pad(expanded, ((0, 0), (1, 1), (0, 0)))
        depthed = gelu_value(depthwise(expand_rim, dw_kernel, RD, WW)).astype(jnp.bfloat16)
        projected = jnp.dot(depthed.reshape(-1, E), project_half, preferred_element_type=jnp.float32).reshape(RD, WW, C)
        return (rows_in[1:-1].astype(jnp.float32) + projected).astype(jnp.bfloat16)
    middle = lax.map(forward_strip, strip_ids).reshape(HH, WW, C)
    middle_values = middle.astype(jnp.float32)
    inverse_two = lax.rsqrt(lax.optimization_barrier(jnp.mean(middle_values * middle_values, axis=-1, keepdims=True)) + epsilon)
    unit_two = middle_values * inverse_two
    normed_two = (unit_two * norm2_gain).astype(jnp.bfloat16)
    block_rows = HH // GRID
    block_cols = WW // GRID

    def into_windows(tokens):
        return tokens.reshape(GRID, block_rows, GRID, block_cols, C).transpose(1, 3, 0, 2, 4).reshape(block_rows, block_cols, GRID * GRID, C)

    def from_windows(windows):
        return windows.reshape(block_rows, block_cols, GRID, GRID, C).transpose(2, 0, 3, 1, 4).reshape(HH, WW, C)
    windows_two = into_windows(normed_two)

    def forward_attend(windows):
        return attend_forward(windows, mixing_half, bias_full, HEADS)[0]
    attended = from_windows(lax.map(forward_attend, windows_two))
    flat_attended = attended.reshape(-1, C)
    flat_cot = cotangent.reshape(-1, C)
    block_out = (middle_values + jnp.dot(flat_attended, output_half, preferred_element_type=jnp.float32).reshape(HH, WW, C)).astype(jnp.bfloat16)
    grad_out = jnp.dot(flat_attended.T, flat_cot, preferred_element_type=jnp.float32) * factor
    grad_attended = jnp.dot(flat_cot, output_half.T, preferred_element_type=jnp.float32).astype(jnp.bfloat16).reshape(HH, WW, C)

    def backward_attend(pieces):
        windows, grad_win = pieces
        attended_win, queries, key_vecs, value_vecs, probability, rounded = attend_forward(windows, mixing_half, bias_full, HEADS)
        return attend_backward(windows, grad_win, mixing_half, queries, key_vecs, value_vecs, probability, rounded, HEADS)
    grad_windows, weight_parts, score_parts = lax.map(backward_attend, (windows_two, into_windows(grad_attended)))
    grad_normed_two = from_windows(grad_windows).astype(jnp.float32)
    grad_qkv = lax.optimization_barrier(jnp.sum(weight_parts, axis=0)) * factor
    grad_bias = jnp.dot(lax.optimization_barrier(jnp.sum(score_parts, axis=0)).reshape(HEADS, -1), onehot, precision=lax.Precision.HIGHEST) * factor
    grad_gain2 = lax.optimization_barrier(jnp.sum(grad_normed_two * unit_two, axis=(0, 1))) * factor
    scaled_two = grad_normed_two * norm2_gain
    grad_middle = (cotangent.astype(jnp.float32) + inverse_two * (scaled_two - unit_two * lax.optimization_barrier(jnp.mean(scaled_two * unit_two, axis=-1, keepdims=True)))).astype(jnp.bfloat16)
    padded_grad = jnp.pad(grad_middle, ((1, 1), (0, 0), (0, 0)))

    def backward_strip(strip_index):
        first_row = (strip_index * RD).astype(jnp.int32)
        rows_in = lax.dynamic_slice_in_dim(padded_image, first_row, RD + 4, 0)
        inverse, unit_form, normed, before, expanded = expand_part(rows_in, norm1_gain, expand_half)
        expand_rim = jnp.pad(expanded, ((0, 0), (1, 1), (0, 0)))
        depth_before = depthwise(expand_rim, dw_kernel, RD + 2, WW)
        depthed = gelu_value(depth_before[1:-1]).astype(jnp.bfloat16)
        grad_rows = lax.dynamic_slice_in_dim(padded_grad, first_row, RD + 2, 0)
        grad_depthed = jnp.dot(grad_rows.reshape(-1, C), project_half.T, preferred_element_type=jnp.float32).reshape(RD + 2, WW, E)
        grad_before = (grad_depthed * gelu_slope(depth_before)).astype(jnp.bfloat16)
        own_grad = grad_before[1:-1].astype(jnp.float32)
        grad_project = jnp.dot(depthed.reshape(-1, E).T, grad_rows[1:-1].reshape(-1, C), preferred_element_type=jnp.float32)
        grad_kernel = jnp.stack([lax.optimization_barrier(jnp.sum(expand_rim[1 + offset // 3:1 + offset // 3 + RD, offset % 3:offset % 3 + WW].astype(jnp.float32) * own_grad, axis=(0, 1))) for offset in range(9)])
        grad_rim = jnp.pad(grad_before, ((0, 0), (1, 1), (0, 0)))
        grad_expanded = depthwise(grad_rim, dw_kernel[::-1], RD, WW)
        grad_expand_before = (grad_expanded * gelu_slope(before[2:-2])).astype(jnp.bfloat16)
        grad_expand = jnp.dot(normed[2:-2].reshape(-1, C).T, grad_expand_before.reshape(-1, E), preferred_element_type=jnp.float32)
        grad_normed = jnp.dot(grad_expand_before.reshape(-1, E), expand_half.T, preferred_element_type=jnp.float32).reshape(RD, WW, C)
        own_unit = unit_form[2:-2]
        scaled = grad_normed * norm1_gain
        grad_gain = lax.optimization_barrier(jnp.sum(grad_normed * own_unit, axis=(0, 1)))
        grad_tile = grad_rows[1:-1].astype(jnp.float32) + inverse[2:-2] * (scaled - own_unit * lax.optimization_barrier(jnp.mean(scaled * own_unit, axis=-1, keepdims=True)))
        return (grad_tile.astype(jnp.bfloat16), grad_gain, grad_expand, grad_kernel, grad_project)
    grad_tiles, gain_parts, expand_parts, kernel_parts, project_parts = lax.map(backward_strip, strip_ids)
    return (block_out, grad_tiles.reshape(HH, WW, C), lax.optimization_barrier(jnp.sum(gain_parts, axis=0)) * factor, lax.optimization_barrier(jnp.sum(expand_parts, axis=0)) * factor, lax.optimization_barrier(jnp.sum(kernel_parts, axis=0)) * factor, lax.optimization_barrier(jnp.sum(project_parts, axis=0)) * factor, grad_gain2, grad_qkv, grad_out, grad_bias)
```

```python
import math

import jax
import jax.numpy as jnp
import numpy as np
from jax import lax
from jax.experimental import pallas as pl
from jax.experimental.pallas import tpu as pltpu
from jax.sharding import Mesh
from jax.sharding import PartitionSpec as P

GRID = 8
C = 128
E = 512
HEADS = 4
RD = 32
CD = 64
LANES = 128
GROUPS = E // LANES
epsilon = 1e-06
gelu_coef = math.sqrt(2.0 / math.pi)
bf16 = jnp.bfloat16
f32 = jnp.float32
VMEM_LIMIT = 50 * 1024 * 1024

PLANE = ("rows", "group")
COLS = ("group", "plane")
ALL = ("rows", "group", "plane")

ROW_EXPAND = 0
ROW_PROJECT = 512
ROW_QKV = 1024
ROW_OUT = 1408
ROW_KERNEL = 1536
ROW_BIAS = 1600
ROWS_USED = 1616
PACK_ROWS = 2048

NT = (((1,), (1,)), ((), ()))
TN = (((0,), (0,)), ((), ()))


def dot(a, b, dims=(((1,), (0,)), ((), ()))):
    return lax.dot_general(a, b, dims, preferred_element_type=f32)


def gelu_value(t):
    t2 = t * t
    u = jnp.tanh(t * (t2 * (0.044715 * gelu_coef) + gelu_coef))
    return t * (0.5 * u + 0.5)


def gelu_pair(t):
    t2 = t * t
    u = jnp.tanh(t * (t2 * (0.044715 * gelu_coef) + gelu_coef))
    h = 0.5 * u + 0.5
    value = t * h
    slope = h + value * (1.0 - h) * (t2 * (2.0 * 0.134145 * gelu_coef) + 2.0 * gelu_coef)
    return value, slope


def normalise(v):
    inverse = lax.rsqrt(jnp.mean(v * v, axis=-1, keepdims=True) + epsilon)
    return inverse, v * inverse


def lane_group(g):
    return slice(g * LANES, (g + 1) * LANES)


def to_columns_kernel(x_ref, o_ref, rows):
    rows[...] = x_ref[...].reshape(RD * CD, C).astype(f32)
    for col in range(CD):
        part = rows[pl.ds(col, RD, stride=CD), :]
        o_ref[col // 2, (col % 2) * RD : (col % 2 + 1) * RD, :] = part.astype(bf16)


def to_columns(x):
    return pl.pallas_call(
        to_columns_kernel,
        out_shape=jax.ShapeDtypeStruct((CD // 2, 2 * RD, C), bf16),
        scratch_shapes=[pltpu.VMEM((RD * CD, C), f32)],
        compiler_params=pltpu.CompilerParams(vmem_limit_bytes=VMEM_LIMIT),
        cost_estimate=pl.CostEstimate(flops=0, bytes_accessed=4 * RD * CD * C, transcendentals=0),
        name="to_columns",
    )(x)


def from_columns_kernel(x_ref, o_ref, cols):
    cols[...] = x_ref[...].reshape(RD * CD, C).astype(f32)
    for row in range(RD):
        o_ref[row, :, :] = cols[pl.ds(row, CD, stride=RD), :].astype(bf16)


def from_columns(x):
    return pl.pallas_call(
        from_columns_kernel,
        out_shape=jax.ShapeDtypeStruct((RD, CD, C), bf16),
        scratch_shapes=[pltpu.VMEM((RD * CD, C), f32)],
        compiler_params=pltpu.CompilerParams(vmem_limit_bytes=VMEM_LIMIT),
        cost_estimate=pl.CostEstimate(flops=0, bytes_accessed=4 * RD * CD * C, transcendentals=0),
        name="from_columns",
    )(x)


def expand_kernel(x_ref, gain_ref, w_ref, e_ref, s_ref, n_ref):
    def step(i, carry):
        at = pl.ds(pl.multiple_of(i * 256, 256), 256)
        normed = (normalise(x_ref[at, :].astype(f32))[1] * gain_ref[...]).astype(bf16)
        n_ref[at, :] = normed
        for g in range(GROUPS):
            value, slope = gelu_pair(dot(normed, w_ref[:, lane_group(g)]))
            e_ref[at, lane_group(g)] = value.astype(bf16)
            s_ref[at, lane_group(g)] = slope.astype(bf16)
        return carry

    lax.fori_loop(0, x_ref.shape[0] // 256, step, 0)


def expand(x, gain, w):
    tokens = x.shape[0]
    block = 512
    wide = pl.BlockSpec((block, E), lambda i: (i, 0))
    slim = pl.BlockSpec((block, C), lambda i: (i, 0))
    return pl.pallas_call(
        expand_kernel,
        grid=(tokens // block,),
        in_specs=[
            slim,
            pl.BlockSpec((1, C), lambda i: (0, 0)),
            pl.BlockSpec((C, E), lambda i: (0, 0)),
        ],
        out_specs=[wide, wide, slim],
        out_shape=[
            jax.ShapeDtypeStruct((tokens, E), bf16),
            jax.ShapeDtypeStruct((tokens, E), bf16),
            jax.ShapeDtypeStruct((tokens, C), bf16),
        ],
        compiler_params=pltpu.CompilerParams(vmem_limit_bytes=VMEM_LIMIT),
        cost_estimate=pl.CostEstimate(
            flops=2 * tokens * C * E + 20 * tokens * E,
            bytes_accessed=tokens * (4 * E + 4 * C),
            transcendentals=tokens * E,
        ),
        name="expand",
    )(x, gain, w)


def conv_row(src, taps, g, row):
    total = None
    for a in range(3):
        for b in range(3):
            term = taps[3 * a + b] * src[g, row + a, 15 + b : 15 + b + CD, :]
            total = term if total is None else total + term
    return total


def depth_kernel(
    e_ref,
    x_ref,
    halo_ref,
    strip_ref,
    gain_ref,
    w1_ref,
    dw_ref,
    w2_ref,
    send_ref,
    d_ref,
    s_ref,
    ss_ref,
    ext,
    side,
    mid,
):
    gain = gain_ref[...]
    halo = normalise(halo_ref[...].reshape(4 * CD, C).astype(f32))[1]
    halo = (halo * gain).astype(bf16)
    strip = normalise(strip_ref[...].reshape(6 * 48, C).astype(f32))[1]
    strip = (strip * gain).astype(bf16)
    for g in range(GROUPS):
        weight = w1_ref[:, lane_group(g)]
        value = gelu_value(dot(halo, weight)).astype(bf16).astype(f32).reshape(4, CD, C)
        for k, row in enumerate((0, 1, RD + 2, RD + 3)):
            ext[g, row, 16 : 16 + CD, :] = value[k]
        value = gelu_value(dot(strip, weight)).astype(bf16).astype(f32).reshape(6, 48, C)
        side[g, :, 0:48, :] = value
        side[g, :, 48:56, :] = jnp.zeros((6, 8, C), f32)
        for row in range(RD + 4):
            ext[g, row, 15:16, :] = value[1, row : row + 1]
            ext[g, row, 16 + CD : 17 + CD, :] = value[4, row : row + 1]

    def fill(row, carry):
        for g in range(GROUPS):
            ext[g, row + 2, 16 : 16 + CD, :] = e_ref[row, :, lane_group(g)].astype(f32)
        return carry

    lax.fori_loop(0, RD, fill, 0)

    def taps_of(g):
        return [dw_ref[t : t + 1, lane_group(g)] for t in range(9)]

    def block(i, carry):
        for k in range(4):
            row = i * 4 + k
            at = pl.ds(pl.multiple_of(row * CD, CD), CD)
            ring = pl.ds(pl.multiple_of(row * CD + CD, CD), CD)
            for g in range(GROUPS):
                value, slope = gelu_pair(conv_row(ext, taps_of(g), g, row + 1))
                d_ref[at, lane_group(g)] = value.astype(bf16)
                s_ref[ring, lane_group(g)] = slope.astype(bf16)
        four = pl.ds(pl.multiple_of(i * 4 * CD, 4 * CD), 4 * CD)
        mid[four, :] = x_ref[four, :].astype(f32) + dot(d_ref[four, :], w2_ref[...])
        return carry

    lax.fori_loop(0, RD // 4, block, 0)
    for g in range(GROUPS):
        taps = taps_of(g)
        for row in (0, RD + 1):
            slope = gelu_pair(conv_row(ext, taps, g, row))[1]
            s_ref[row * CD : (row + 1) * CD, lane_group(g)] = slope.astype(bf16)
        for end in range(2):
            total = None
            for a in range(3):
                for b in range(3):
                    term = taps[3 * a + b] * side[g, 3 * end + b, a : a + 48, :]
                    total = term if total is None else total + term
            ss_ref[end, :, lane_group(g)] = gelu_pair(total)[1].astype(bf16)
    for col in range(CD):
        part = mid[pl.ds(col, RD, stride=CD), :]
        send_ref[col // 2, (col % 2) * RD : (col % 2 + 1) * RD, :] = part.astype(bf16)


def depth(expanded, x, halo, strip, gain, w1, taps, w2):
    tokens = RD * CD
    return pl.pallas_call(
        depth_kernel,
        out_shape=[
            jax.ShapeDtypeStruct((CD // 2, 2 * RD, C), bf16),
            jax.ShapeDtypeStruct((tokens, E), bf16),
            jax.ShapeDtypeStruct((tokens + 2 * CD, E), bf16),
            jax.ShapeDtypeStruct((2, 48, E), bf16),
        ],
        scratch_shapes=[
            pltpu.VMEM((GROUPS, RD + 4, 96, LANES), f32),
            pltpu.VMEM((GROUPS, 6, 56, LANES), f32),
            pltpu.VMEM((tokens, C), f32),
        ],
        compiler_params=pltpu.CompilerParams(vmem_limit_bytes=VMEM_LIMIT),
        cost_estimate=pl.CostEstimate(
            flops=2 * tokens * C * E + 40 * tokens * E,
            bytes_accessed=tokens * (6 * E + 4 * C),
            transcendentals=tokens * E,
        ),
        name="depth",
    )(expanded.reshape(RD, CD, E), x, halo, strip, gain, w1, taps, w2)


def side_by_side(x):
    return jnp.concatenate([x[:64], x[64:]], axis=1)


def stacked(x):
    return jnp.concatenate([x[:, :C], x[:, C:]], axis=0)


def diagonal(x):
    return jnp.concatenate([x[:64, :C], x[64:, C:]], axis=0)


def attend_kernel(
    m_ref,
    c_ref,
    gain_ref,
    wq_ref,
    wo_ref,
    bias_ref,
    bo_ref,
    gm_ref,
    gq_ref,
    go_ref,
    ds_ref,
    mid,
    cot,
    out,
    grad,
    norms,
    atts,
    cots,
    mixes,
):
    mid[...] = m_ref[...].reshape(RD * CD, C).astype(f32)
    cot[...] = c_ref[...].reshape(RD * CD, C).astype(f32)
    grad[...] = jnp.zeros(grad.shape, f32)
    ds_ref[...] = jnp.zeros(ds_ref.shape, f32)
    gain = gain_ref[...]
    scale = 32**-0.5
    row_head = lax.broadcasted_iota(jnp.int32, (256, 256), 0) // 64
    lane_head = (lax.broadcasted_iota(jnp.int32, (256, 256), 1) % C) // 32
    own_head = row_head == lane_head
    fold_head = (lax.broadcasted_iota(jnp.int32, (64, 256), 1) % C) // 32

    def per_head(x):
        x = side_by_side(x)
        x = jnp.concatenate([x, x, x, x], axis=0)
        return jnp.where(own_head, x, jnp.zeros_like(x))

    def per_window(x):
        none = jnp.zeros((64, C), x.dtype)
        top = jnp.concatenate([x[:64], none], axis=1)
        low = jnp.concatenate([none, x[64:]], axis=1)
        return jnp.concatenate([top, low], axis=0)

    def fold(x):
        total = x[0:64]
        for h in range(1, HEADS):
            total = jnp.where(fold_head == h, x[h * 64 : (h + 1) * 64], total)
        return stacked(total)

    def windows(src, r0, width, first):
        parts = []
        for c in range(2):
            for il in range(2):
                at = pl.ds(c * (width // 2) + il * 16 + first + r0, 32, stride=width)
                parts.append(src[at, :])
        return jnp.concatenate(parts, axis=0)

    def put(dst, r0, width, first, x):
        for c in range(2):
            for il in range(2):
                at = pl.ds(c * (width // 2) + il * 16 + first + r0, 32, stride=width)
                k = 2 * c + il
                dst[at, :] = x[k * 32 : (k + 1) * 32]

    def pair(r0, carry):
        at = pl.ds(pl.multiple_of(r0 * 128, 128), 128)
        m = windows(mid, r0, 64, 0)
        ct = windows(cot, r0, 64, 0)
        ctb = ct.astype(bf16)
        inverse, unit = normalise(m)
        normed = (unit * gain).astype(bf16)
        mixture = dot(normed, wq_ref[...])
        q = (mixture[:, :C] * scale).astype(bf16)
        k = mixture[:, C : 2 * C].astype(bf16)
        v = mixture[:, 2 * C :].astype(bf16)
        ga = dot(ctb, wo_ref[...], NT).astype(bf16)
        k4 = per_head(k)
        v4 = per_head(v)
        qd = per_window(q)
        gd = per_window(ga)
        scores = (dot(k4, qd, NT) + bias_ref[...]).reshape(HEADS, 64, 128)
        weights = jnp.exp(scores - jnp.max(scores, axis=1, keepdims=True))
        prob = weights * (1.0 / jnp.sum(weights, axis=1, keepdims=True))
        rounded = prob.reshape(256, 128).astype(bf16)
        att = diagonal(dot(rounded, v4, TN)).astype(bf16)
        gp = dot(v4, gd, NT).reshape(HEADS, 64, 128)
        gs = prob * (gp - jnp.sum(prob * gp, axis=1, keepdims=True))
        gs = gs.reshape(256, 128)
        ds_ref[...] += gs
        gr = gs.astype(bf16)
        gv = fold(dot(rounded, gd))
        gk = fold(dot(gr, qd))
        gq = diagonal(dot(gr, k4, TN)) * scale
        gx = jnp.concatenate([gq, gk, gv], axis=1).astype(bf16)
        gn = dot(gx, wq_ref[...], NT).astype(bf16).astype(f32)
        scaled = gn * gain
        gm = ct + inverse * (scaled - unit * jnp.mean(scaled * unit, axis=-1, keepdims=True))
        put(grad, r0, 80, 1, gm)
        put(out, r0, 64, 0, m + dot(att, wo_ref[...]))
        norms[at, :] = normed
        atts[at, :] = att
        cots[at, :] = ctb
        mixes[at, :] = gx
        return carry

    lax.fori_loop(0, 16, pair, 0)
    for k in range(3):
        gq_ref[k * C : (k + 1) * C, :] = dot(norms[...], mixes[:, k * C : (k + 1) * C], TN)
    go_ref[...] = dot(atts[...], cots[...], TN)
    for c in range(2):
        low = grad[pl.ds(c * 40 + 32, 24, stride=80), :]
        high = grad[pl.ds(c * 40 + 1 + 8 * 80, 24, stride=80), :]
        grad[pl.ds(c * 40 + 8 * 80, 24, stride=80), :] = low
        grad[pl.ds(c * 40 + 33, 24, stride=80), :] = high
    bo_ref[...] = out[...].astype(bf16).reshape(bo_ref.shape)
    gm_ref[...] = grad[...].astype(bf16).reshape(gm_ref.shape)


def attend(mid, cot, gain, wq, wo, bias):
    tokens = RD * CD
    return pl.pallas_call(
        attend_kernel,
        out_shape=[
            jax.ShapeDtypeStruct((32, 64, C), bf16),
            jax.ShapeDtypeStruct((32, 80, C), bf16),
            jax.ShapeDtypeStruct((3 * C, C), f32),
            jax.ShapeDtypeStruct((C, C), f32),
            jax.ShapeDtypeStruct((256, 128), f32),
        ],
        scratch_shapes=[
            pltpu.VMEM((tokens, C), f32),
            pltpu.VMEM((tokens, C), f32),
            pltpu.VMEM((tokens, C), f32),
            pltpu.VMEM((32 * 80, C), f32),
            pltpu.VMEM((tokens, C), bf16),
            pltpu.VMEM((tokens, C), bf16),
            pltpu.VMEM((tokens, C), bf16),
            pltpu.VMEM((tokens, 3 * C), bf16),
        ],
        compiler_params=pltpu.CompilerParams(vmem_limit_bytes=VMEM_LIMIT),
        cost_estimate=pl.CostEstimate(
            flops=40 * tokens * C * C, bytes_accessed=tokens * 8 * C, transcendentals=tokens * 256
        ),
        name="attend",
    )(mid, cot, gain, wq, wo, bias)


def project_grad_kernel(g_ref, w2_ref, d_ref, s_ref, b_ref, gp_ref, gm_ref, cols):
    cols[...] = g_ref[...].reshape(CD * 40, C).astype(f32)
    gp_ref[...] = jnp.zeros(gp_ref.shape, f32)

    def rows(first, count):
        parts = [cols[pl.ds(first + k, CD, stride=40), :] for k in range(count)]
        return jnp.concatenate(parts, axis=0).astype(bf16)

    def before(g, at):
        for k in range(GROUPS):
            wide = dot(g, w2_ref[lane_group(k), :], NT)
            wide = wide * s_ref[at, lane_group(k)].astype(f32)
            b_ref[at, lane_group(k)] = wide.astype(bf16)

    def block(i, carry):
        four = pl.ds(pl.multiple_of(i * 4 * CD, 4 * CD), 4 * CD)
        ring = pl.ds(pl.multiple_of(i * 4 * CD + CD, CD), 4 * CD)
        g = rows(i * 4 + 1, 4)
        gm_ref[four, :] = g
        before(g, ring)
        for k in range(GROUPS):
            gp_ref[lane_group(k), :] += dot(g, d_ref[four, lane_group(k)], TN)
        return carry

    lax.fori_loop(0, RD // 4, block, 0)
    for row in (0, RD + 1):
        before(rows(row, 1), pl.ds(row * CD, CD))


def project_grad(gm, w2, depthed, slope):
    tokens = RD * CD
    return pl.pallas_call(
        project_grad_kernel,
        out_shape=[
            jax.ShapeDtypeStruct((tokens + 2 * CD, E), bf16),
            jax.ShapeDtypeStruct((E, C), f32),
            jax.ShapeDtypeStruct((tokens, C), bf16),
        ],
        scratch_shapes=[pltpu.VMEM((CD * 40, C), f32)],
        compiler_params=pltpu.CompilerParams(vmem_limit_bytes=VMEM_LIMIT),
        cost_estimate=pl.CostEstimate(
            flops=4 * tokens * C * E, bytes_accessed=tokens * (6 * E + 4 * C), transcendentals=0
        ),
        name="project_grad",
    )(gm, w2, depthed, slope)


def depth_grad_kernel(
    b_ref,
    strip_ref,
    ss_ref,
    w2_ref,
    dw_ref,
    e_ref,
    s_ref,
    n_ref,
    gp_ref,
    gq_ref,
    go_ref,
    gb_ref,
    x_ref,
    pack_ref,
    ext,
    sums,
    total,
):
    strip = strip_ref[...].reshape(2 * 48, C)
    for g in range(GROUPS):
        wide = dot(strip, w2_ref[lane_group(g), :], NT).reshape(2, 48, LANES)
        wide = (wide * ss_ref[:, :, lane_group(g)].astype(f32)).astype(bf16).astype(f32)
        for row in range(RD + 2):
            ext[g, row, 15:16, :] = wide[0, row : row + 1]
            ext[g, row, 16 + CD : 17 + CD, :] = wide[1, row : row + 1]

    def fill(row, carry):
        for g in range(GROUPS):
            ext[g, row, 16 : 16 + CD, :] = b_ref[row, :, lane_group(g)].astype(f32)
        return carry

    lax.fori_loop(0, RD + 2, fill, 0)
    sums[...] = jnp.zeros(sums.shape, f32)
    total[...] = jnp.zeros(total.shape, f32)

    def block(i, carry):
        for k in range(4):
            row = i * 4 + k
            at = pl.ds(pl.multiple_of(row * CD, CD), CD)
            for g in range(GROUPS):
                own = e_ref[at, lane_group(g)].astype(f32)
                running = None
                for t in range(9):
                    window = ext[g, row + t // 3, 15 + t % 3 : 15 + t % 3 + CD, :]
                    term = dw_ref[8 - t : 9 - t, lane_group(g)] * window
                    running = term if running is None else running + term
                    sums[g, 8 - t] += jnp.sum((own * window).reshape(CD // 8, 8, LANES), axis=0)
                wide = running * s_ref[at, lane_group(g)].astype(f32)
                x_ref[at, lane_group(g)] = wide.astype(bf16)
        four = pl.ds(pl.multiple_of(i * 4 * CD, 4 * CD), 4 * CD)
        normed = n_ref[four, :]
        for g in range(GROUPS):
            total[lane_group(g), :] += dot(normed, x_ref[four, lane_group(g)], TN)
        return carry

    lax.fori_loop(0, RD // 4, block, 0)
    pack_ref[ROW_EXPAND : ROW_EXPAND + E, :] = total[...].astype(bf16)
    pack_ref[ROW_PROJECT : ROW_PROJECT + E, :] = gp_ref[...].astype(bf16)
    pack_ref[ROW_QKV : ROW_QKV + 3 * C, :] = gq_ref[...].astype(bf16)
    pack_ref[ROW_OUT : ROW_OUT + C, :] = go_ref[...].astype(bf16)
    for g in range(GROUPS):
        kernel_sums = jnp.sum(sums[g], axis=1)
        kernel_sums = jnp.concatenate([kernel_sums, jnp.zeros((7, LANES), f32)], axis=0)
        pack_ref[ROW_KERNEL + 16 * g : ROW_KERNEL + 16 * g + 16, :] = kernel_sums.astype(bf16)
    pack_ref[ROW_BIAS : ROW_BIAS + 16, :] = gb_ref[...].astype(bf16)
    pack_ref[ROWS_USED:PACK_ROWS, :] = jnp.zeros((PACK_ROWS - ROWS_USED, C), bf16)


def depth_grad(before, strip, ss, w2, taps, expanded, slope, normed, gp, gq, go, gb):
    tokens = RD * CD
    return pl.pallas_call(
        depth_grad_kernel,
        out_shape=[
            jax.ShapeDtypeStruct((tokens, E), bf16),
            jax.ShapeDtypeStruct((PACK_ROWS, C), bf16),
        ],
        scratch_shapes=[
            pltpu.VMEM((GROUPS, RD + 2, 96, LANES), f32),
            pltpu.VMEM((GROUPS, 9, 8, LANES), f32),
            pltpu.VMEM((E, C), f32),
        ],
        compiler_params=pltpu.CompilerParams(vmem_limit_bytes=VMEM_LIMIT),
        cost_estimate=pl.CostEstimate(
            flops=2 * tokens * C * E + 60 * tokens * E,
            bytes_accessed=tokens * (8 * E + 4 * C),
            transcendentals=0,
        ),
        name="depth_grad",
    )(
        before.reshape(RD + 2, CD, E), strip, ss, w2, taps, expanded, slope, normed, gp, gq, go, gb
    )


def image_grad_kernel(g_ref, w_ref, gain_ref, x_ref, m_ref, o_ref):
    def step(i, carry):
        at = pl.ds(pl.multiple_of(i * 256, 256), 256)
        scaled = dot(g_ref[at, :], w_ref[...], NT) * gain_ref[...]
        inverse, unit = normalise(x_ref[at, :].astype(f32))
        mean = jnp.mean(scaled * unit, axis=-1, keepdims=True)
        o_ref[at, :] = (m_ref[at, :].astype(f32) + inverse * (scaled - unit * mean)).astype(bf16)
        return carry

    lax.fori_loop(0, x_ref.shape[0] // 256, step, 0)


def image_grad(g, w, gain, x, gm):
    tokens = x.shape[0]
    block = 1024
    slim = pl.BlockSpec((block, C), lambda i: (i, 0))
    return pl.pallas_call(
        image_grad_kernel,
        grid=(tokens // block,),
        in_specs=[
            pl.BlockSpec((block, E), lambda i: (i, 0)),
            pl.BlockSpec((C, E), lambda i: (0, 0)),
            pl.BlockSpec((1, C), lambda i: (0, 0)),
            slim,
            slim,
        ],
        out_specs=slim,
        out_shape=jax.ShapeDtypeStruct((tokens, C), bf16),
        compiler_params=pltpu.CompilerParams(vmem_limit_bytes=VMEM_LIMIT),
        cost_estimate=pl.CostEstimate(
            flops=2 * tokens * C * E, bytes_accessed=tokens * (2 * E + 6 * C), transcendentals=0
        ),
        name="image_grad",
    )(g, w, gain, x, gm)


def sum_parts_kernel(factor, x_ref, o_ref):
    total = x_ref[0].astype(f32)
    for k in range(1, x_ref.shape[0]):
        total = total + x_ref[k].astype(f32)
    total = (total * factor).astype(bf16)
    for k in range(x_ref.shape[0]):
        o_ref[k] = total


def sum_parts(x, factor):
    return pl.pallas_call(
        lambda x_ref, o_ref: sum_parts_kernel(factor, x_ref, o_ref),
        out_shape=jax.ShapeDtypeStruct(x.shape, bf16),
        compiler_params=pltpu.CompilerParams(vmem_limit_bytes=VMEM_LIMIT),
        cost_estimate=pl.CostEstimate(
            flops=2 * x.size, bytes_accessed=4 * x.size, transcendentals=0
        ),
        name="sum_parts",
    )(x)


def column_sums(x):
    line = jnp.sum(x, axis=1, keepdims=True)
    return jnp.broadcast_to(line, (C, C)).T[0:1]


def unpack_kernel(
    p_ref, w1_ref, wq_ref, gain1_ref, gain2_ref, g1_ref, ex_ref, k_ref, pr_ref, g2_ref, qk_ref,
    o_ref, b_ref
):
    first = jnp.zeros((C, C), f32)
    second = jnp.zeros((C, C), f32)
    for g in range(GROUPS):
        part = p_ref[ROW_EXPAND + g * C : ROW_EXPAND + (g + 1) * C, :].astype(f32)
        ex_ref[:, lane_group(g)] = part
        first = first + part * w1_ref[:, lane_group(g)].astype(f32)
        part = p_ref[ROW_PROJECT + g * C : ROW_PROJECT + (g + 1) * C, :].astype(f32)
        pr_ref[g * C : (g + 1) * C, :] = part.T
        part = p_ref[ROW_KERNEL + g * 16 : ROW_KERNEL + (g + 1) * 16, :].astype(f32)
        k_ref[:, lane_group(g)] = part[0:9]
    for k in range(3):
        part = p_ref[ROW_QKV + k * C : ROW_QKV + (k + 1) * C, :].astype(f32)
        qk_ref[:, lane_group(k)] = part
        second = second + part * wq_ref[:, lane_group(k)].astype(f32)
    g1_ref[...] = column_sums(first) / gain1_ref[...]
    g2_ref[...] = column_sums(second) / gain2_ref[...]
    o_ref[...] = p_ref[ROW_OUT : ROW_OUT + C, :].astype(f32)
    part = p_ref[ROW_BIAS : ROW_BIAS + 16, :].astype(f32)
    b_ref[...] = jnp.concatenate([part[0:4], part[4:8]], axis=1)[:, :225]


def unpack(pack, w1, wq, gain1, gain2):
    return pl.pallas_call(
        unpack_kernel,
        out_shape=[
            jax.ShapeDtypeStruct((1, C), f32),
            jax.ShapeDtypeStruct((C, E), f32),
            jax.ShapeDtypeStruct((9, E), f32),
            jax.ShapeDtypeStruct((E, C), f32),
            jax.ShapeDtypeStruct((1, C), f32),
            jax.ShapeDtypeStruct((C, 3 * C), f32),
            jax.ShapeDtypeStruct((C, C), f32),
            jax.ShapeDtypeStruct((HEADS, 225), f32),
        ],
        compiler_params=pltpu.CompilerParams(vmem_limit_bytes=VMEM_LIMIT),
        cost_estimate=pl.CostEstimate(
            flops=4 * pack.size, bytes_accessed=6 * pack.size, transcendentals=0
        ),
        name="unpack",
    )(pack, w1, wq, gain1, gain2)


def pair_onehot():
    place = np.arange(64)
    row = 2 * ((place % 32) // 8) + place // 32
    col = place % 8
    first, second = place[None, :], place[:, None]
    index = 15 * (row[first] - row[second] + 7) + col[first] - col[second] + 7
    index = jnp.asarray(np.concatenate([index, index], axis=1), jnp.int32)
    return (index[:, :, None] == jnp.arange(225, dtype=jnp.int32)).astype(f32)


def per_device(
    image,
    cotangent,
    norm1_gain,
    w_expand,
    dw_kernel,
    w_project,
    norm2_gain,
    w_qkv,
    w_out,
    bias_table,
):
    factor = 1.0 / math.sqrt(RD * CD * 128)
    w1 = w_expand.astype(bf16)
    w2 = w_project.astype(bf16)
    wq = w_qkv.astype(bf16)
    wo = w_out.astype(bf16)
    gain1 = norm1_gain.reshape(1, C)
    gain2 = norm2_gain.reshape(1, C)
    onehot = pair_onehot()
    bias = jnp.einsum("hq,jlq->hjl", bias_table, onehot, precision=lax.Precision.HIGHEST)
    bias = bias.reshape(HEADS * 64, 128)

    row_up = [(i, i + 1) for i in range(3)]
    row_down = [(i + 1, i) for i in range(3)]
    col_up = [(i, i + 1) for i in range(31)]
    col_down = [(i + 1, i) for i in range(31)]

    above = lax.ppermute(image[RD - 2 :], "rows", row_up)
    below = lax.ppermute(image[:2], "rows", row_down)
    cot_windows = lax.all_to_all(to_columns(cotangent), PLANE, 0, 0, tiled=True)
    tokens = image.reshape(RD * CD, C)
    expanded, slope1, normed1 = expand(tokens, gain1, w1)

    halo = jnp.concatenate([above, below], axis=0)
    left = jnp.concatenate([above[:, :2], image[:, :2], below[:, :2]], axis=0)
    right = jnp.concatenate([above[:, -2:], image[:, -2:], below[:, -2:]], axis=0)
    left = left.transpose(1, 0, 2)
    right = right.transpose(1, 0, 2)
    before_left = lax.ppermute(right, COLS, col_up)
    after_right = lax.ppermute(left, COLS, col_down)
    strip = jnp.concatenate([before_left, left[:1], right[1:], after_right], axis=0)
    strip = jnp.pad(strip, ((0, 0), (0, 12), (0, 0)))
    send, depthed, slope2, slope2_strip = depth(
        expanded, tokens, halo, strip, gain1, w1, dw_kernel, w2
    )

    mid_windows = lax.all_to_all(send, PLANE, 0, 0, tiled=True)
    out_windows, grad_windows, grad_qkv, grad_out, score_sums = attend(
        mid_windows, cot_windows, gain2, wq, wo, bias
    )
    grad_cols = lax.all_to_all(grad_windows, PLANE, 0, 0, tiled=True)
    grad_left = lax.ppermute(grad_cols[31, 40:], COLS, col_up)
    grad_right = lax.ppermute(grad_cols[0, :40], COLS, col_down)
    before, grad_project, grad_middle = project_grad(grad_cols, w2, depthed, slope2)
    grad_strip = jnp.pad(jnp.stack([grad_left, grad_right]), ((0, 0), (0, 8), (0, 0)))

    grad_bias = jnp.einsum(
        "hjl,jlq->hq",
        score_sums.reshape(HEADS, 64, 128),
        onehot,
        precision=lax.Precision.HIGHEST,
    )
    grad_bias = jnp.pad(grad_bias, ((0, 0), (0, 31)))
    grad_bias = jnp.concatenate([grad_bias[:, :128], grad_bias[:, 128:]], axis=0)
    grad_bias = jnp.pad(grad_bias, ((0, 8), (0, 0)))
    block_cols = lax.all_to_all(out_windows, PLANE, 0, 0, tiled=True)

    grad_wide, pack = depth_grad(
        before, grad_strip, slope2_strip, w2, dw_kernel, expanded, slope1, normed1,
        grad_project, grad_qkv, grad_out, grad_bias,
    )
    parts = lax.all_to_all(pack.reshape(128, 16, C), ALL, 0, 0, tiled=True)
    grad_image = image_grad(grad_wide, w1, gain1, tokens, grad_middle)
    block_out = from_columns(block_cols)
    whole = lax.all_to_all(sum_parts(parts, factor), ALL, 0, 0, tiled=True)
    g1, ge, gk, gp, g2, gq, go, gb = unpack(whole.reshape(PACK_ROWS, C), w1, wq, gain1, gain2)
    return (
        block_out,
        grad_image.reshape(RD, CD, C),
        g1.reshape(C),
        ge,
        gk,
        gp,
        g2.reshape(C),
        gq,
        go,
        gb,
    )


def solution(mesh):
    mesh = Mesh(mesh.devices.reshape(4, 8, 4), ALL)
    tiles = P("rows", COLS, None)
    return jax.shard_map(
        per_device,
        mesh=mesh,
        in_specs=(tiles, tiles) + (P(),) * 8,
        out_specs=(tiles, tiles) + (P(),) * 8,
        check_vma=False,
    )
```

```python
import math

import jax
import jax.numpy as jnp
import numpy as np
from jax import lax
from jax.experimental import pallas as pl
from jax.experimental.pallas import tpu as pltpu
from jax.sharding import Mesh
from jax.sharding import PartitionSpec as P

GRID = 8
C = 128
E = 512
HEADS = 4
RD = 32
CD = 64
LANES = 128
GROUPS = E // LANES
epsilon = 1e-06
gelu_coef = math.sqrt(2.0 / math.pi)
bf16 = jnp.bfloat16
f32 = jnp.float32
VMEM_LIMIT = 24 * 1024 * 1024

PLANE = ("rows", "group")
COLS = ("group", "plane")
ALL = ("rows", "group", "plane")

ROW_EXPAND = 0
ROW_PROJECT = 512
ROW_QKV = 1024
ROW_OUT = 1408
ROW_KERNEL = 1536
ROW_BIAS = 1600
ROWS_USED = 1616
PACK_ROWS = 2048

PAIRS = 4

HBM = pl.BlockSpec(memory_space=pltpu.HBM)
ANY = pl.BlockSpec()
NT = (((1,), (1,)), ((), ()))
TN = (((0,), (0,)), ((), ()))


def dot(a, b, dims=(((1,), (0,)), ((), ()))):
    return lax.dot_general(a, b, dims, preferred_element_type=f32)


def gelu_value(t):
    t2 = t * t
    u = jnp.tanh(t * (t2 * (0.044715 * gelu_coef) + gelu_coef))
    return t * (0.5 * u + 0.5)


def gelu_pair(t):
    t2 = t * t
    u = jnp.tanh(t * (t2 * (0.044715 * gelu_coef) + gelu_coef))
    h = 0.5 * u + 0.5
    value = t * h
    slope = h + value * (1.0 - h) * (t2 * (2.0 * 0.134145 * gelu_coef) + 2.0 * gelu_coef)
    return value, slope


def normalise(v):
    inverse = lax.rsqrt(jnp.mean(v * v, axis=-1, keepdims=True) + epsilon)
    return inverse, v * inverse


def rows_of(i, count):
    return pl.ds(pl.multiple_of(i * count, count), count)


def copies(pairs, sems):
    return [pltpu.make_async_copy(a, b, sems.at[k]) for k, (a, b) in enumerate(pairs)]


class Blocks:
    def __init__(self, src, dst, sems, count):
        self.src, self.dst, self.sems, self.count = src, dst, sems, count
        self.steps = src.shape[0] // count

    def copy(self, i):
        at = rows_of(i, self.count) if not isinstance(i, int) else pl.ds(i * self.count, self.count)
        return pltpu.make_async_copy(self.src.at[at], self.dst.at[at], self.sems.at[i])

    def start_all(self):
        for i in range(self.steps):
            self.copy(i).start()

    def wait_all(self):
        for i in range(self.steps):
            self.copy(i).wait()


def lane_group(g):
    return slice(g * LANES, (g + 1) * LANES)


def to_columns_kernel(x_ref, o_ref, rows):
    rows[...] = x_ref[...].reshape(RD * CD, C).astype(f32)
    for col in range(CD):
        part = rows[pl.ds(col, RD, stride=CD), :]
        o_ref[col // 2, (col % 2) * RD : (col % 2 + 1) * RD, :] = part.astype(bf16)


def to_columns(x):
    return pl.pallas_call(
        to_columns_kernel,
        out_shape=jax.ShapeDtypeStruct((CD // 2, 2 * RD, C), bf16),
        scratch_shapes=[pltpu.VMEM((RD * CD, C), f32)],
        compiler_params=pltpu.CompilerParams(vmem_limit_bytes=VMEM_LIMIT),
        cost_estimate=pl.CostEstimate(flops=0, bytes_accessed=4 * RD * CD * C, transcendentals=0),
        name="to_columns",
    )(x)


def from_columns_kernel(x_ref, o_ref, cols):
    cols[...] = x_ref[:, 80:144, :].reshape(RD * CD, C).astype(f32)
    for row in range(RD):
        o_ref[row, :, :] = cols[pl.ds(row, CD, stride=RD), :].astype(bf16)


def from_columns(x):
    return pl.pallas_call(
        from_columns_kernel,
        out_shape=jax.ShapeDtypeStruct((RD, CD, C), bf16),
        scratch_shapes=[pltpu.VMEM((RD * CD, C), f32)],
        compiler_params=pltpu.CompilerParams(vmem_limit_bytes=VMEM_LIMIT),
        cost_estimate=pl.CostEstimate(flops=0, bytes_accessed=4 * RD * CD * C, transcendentals=0),
        name="from_columns",
    )(x)


def expand_kernel(x_ref, gain_ref, w_ref, e_ref, s_ref, n_ref):
    w = w_ref[...].astype(bf16)

    def step(i, carry):
        at = pl.ds(pl.multiple_of(i * 256, 256), 256)
        normed = (normalise(x_ref[at, :].astype(f32))[1] * gain_ref[...]).astype(bf16)
        n_ref[at, :] = normed
        for g in range(GROUPS):
            value, slope = gelu_pair(dot(normed, w[:, lane_group(g)]))
            e_ref[at, lane_group(g)] = value.astype(bf16)
            s_ref[at, lane_group(g)] = slope.astype(bf16)
        return carry

    lax.fori_loop(0, x_ref.shape[0] // 256, step, 0)


def expand(x, gain, w):
    tokens = x.shape[0]
    return pl.pallas_call(
        expand_kernel,
        out_shape=[
            jax.ShapeDtypeStruct((tokens, E), bf16),
            jax.ShapeDtypeStruct((tokens, E), bf16),
            jax.ShapeDtypeStruct((tokens, C), bf16),
        ],
        compiler_params=pltpu.CompilerParams(vmem_limit_bytes=VMEM_LIMIT),
        cost_estimate=pl.CostEstimate(
            flops=2 * tokens * C * E + 20 * tokens * E,
            bytes_accessed=tokens * (4 * E + 4 * C),
            transcendentals=tokens * E,
        ),
        name="expand",
    )(x, gain, w)


def conv_row(src, taps, g, row):
    total = None
    for a in range(3):
        for b in range(3):
            term = taps[3 * a + b] * src[g, row + a, 15 + b : 15 + b + CD, :]
            total = term if total is None else total + term
    return total


def depth_kernel(
    e_ref,
    x_ref,
    c_ref,
    halo_ref,
    strip_ref,
    gain_ref,
    w1_ref,
    dw_ref,
    w2f_ref,
    send_ref,
    d_ref,
    s_ref,
    ss_ref,
    ext,
    side,
    mid,
    w2_ref,
):
    w2_ref[...] = w2f_ref[...].astype(bf16)
    send_ref[:, 64:128, :] = c_ref[...]
    gain = gain_ref[...]
    halo = normalise(halo_ref[...].reshape(4 * CD, C).astype(f32))[1]
    halo = (halo * gain).astype(bf16)
    strip = normalise(strip_ref[...].reshape(6 * 48, C).astype(f32))[1]
    strip = (strip * gain).astype(bf16)
    for g in range(GROUPS):
        weight = w1_ref[:, lane_group(g)].astype(bf16)
        value = gelu_value(dot(halo, weight)).astype(bf16).astype(f32).reshape(4, CD, C)
        for k, row in enumerate((0, 1, RD + 2, RD + 3)):
            ext[g, row, 16 : 16 + CD, :] = value[k]
        value = gelu_value(dot(strip, weight)).astype(bf16).astype(f32).reshape(6, 48, C)
        side[g, :, 0:48, :] = value
        side[g, :, 48:56, :] = jnp.zeros((6, 8, C), f32)
        for row in range(RD + 4):
            ext[g, row, 15:16, :] = value[1, row : row + 1]
            ext[g, row, 16 + CD : 17 + CD, :] = value[4, row : row + 1]

    def fill(i):
        for k in range(4):
            row = i * 4 + k
            for g in range(GROUPS):
                ext[g, row + 2, 16 : 16 + CD, :] = e_ref[row, :, lane_group(g)].astype(f32)

    def taps_of(g):
        return [dw_ref[t : t + 1, lane_group(g)] for t in range(9)]

    fill(0)

    def block(i, carry):
        @pl.when(i < RD // 4 - 1)
        def _():
            fill(i + 1)

        for k in range(4):
            row = i * 4 + k
            at = pl.ds(pl.multiple_of(row * CD, CD), CD)
            ring = pl.ds(pl.multiple_of(row * CD + CD, CD), CD)
            for g in range(GROUPS):
                value, slope = gelu_pair(conv_row(ext, taps_of(g), g, row + 1))
                d_ref[at, lane_group(g)] = value.astype(bf16)
                s_ref[ring, lane_group(g)] = slope.astype(bf16)
        four = pl.ds(pl.multiple_of(i * 4 * CD, 4 * CD), 4 * CD)
        mid[four, :] = x_ref[four, :].astype(f32) + dot(d_ref[four, :], w2_ref[...])
        return carry

    lax.fori_loop(0, RD // 4, block, 0)
    for col in range(CD):
        part = mid[pl.ds(col, RD, stride=CD), :]
        send_ref[col // 2, (col % 2) * RD : (col % 2 + 1) * RD, :] = part.astype(bf16)
    for g in range(GROUPS):
        taps = taps_of(g)
        for row in (0, RD + 1):
            slope = gelu_pair(conv_row(ext, taps, g, row))[1]
            s_ref[row * CD : (row + 1) * CD, lane_group(g)] = slope.astype(bf16)
        for end in range(2):
            total = None
            for a in range(3):
                for b in range(3):
                    term = taps[3 * a + b] * side[g, 3 * end + b, a : a + 48, :]
                    total = term if total is None else total + term
            ss_ref[end, :, lane_group(g)] = gelu_pair(total)[1].astype(bf16)


def depth(expanded, x, cot, halo, strip, gain, w1, taps, w2):
    tokens = RD * CD
    return pl.pallas_call(
        depth_kernel,
        out_shape=[
            jax.ShapeDtypeStruct((CD // 2, 4 * RD, C), bf16),
            jax.ShapeDtypeStruct((tokens, E), bf16),
            jax.ShapeDtypeStruct((tokens + 2 * CD, E), bf16),
            jax.ShapeDtypeStruct((2, 48, E), bf16),
        ],
        scratch_shapes=[
            pltpu.VMEM((GROUPS, RD + 4, 96, LANES), f32),
            pltpu.VMEM((GROUPS, 6, 56, LANES), f32),
            pltpu.VMEM((tokens, C), f32),
            pltpu.VMEM((E, C), bf16),
        ],
        compiler_params=pltpu.CompilerParams(vmem_limit_bytes=VMEM_LIMIT),
        cost_estimate=pl.CostEstimate(
            flops=2 * tokens * C * E + 40 * tokens * E,
            bytes_accessed=tokens * (6 * E + 4 * C),
            transcendentals=tokens * E,
        ),
        name="depth",
    )(expanded.reshape(RD, CD, E), x, cot, halo, strip, gain, w1, taps, w2)


def side_by_side(x):
    return jnp.concatenate([x[:64], x[64:]], axis=1)


def stacked(x):
    return jnp.concatenate([x[:, :C], x[:, C:]], axis=0)


def diagonal(x):
    return jnp.concatenate([x[:64, :C], x[64:, C:]], axis=0)


def attend_kernel(
    x_ref,
    gain_ref,
    wqf_ref,
    wof_ref,
    bias_ref,
    back_ref,
    gq_ref,
    go_ref,
    gb_ref,
    mid,
    cot,
    out,
    grad,
    norms,
    atts,
    cots,
    mixes,
    ds_ref,
    wq_ref,
    wo_ref,
):
    grad[...] = jnp.zeros(grad.shape, f32)
    ds_ref[...] = jnp.zeros(ds_ref.shape, f32)
    wq_ref[...] = wqf_ref[...].astype(bf16)
    wo_ref[...] = wof_ref[...].astype(bf16)
    mid[...] = x_ref[:, 0:64, :].reshape(RD * CD, C).astype(f32)
    cot[...] = x_ref[:, 64:128, :].reshape(RD * CD, C).astype(f32)
    gain = gain_ref[...]
    scale = 32**-0.5
    row_head = lax.broadcasted_iota(jnp.int32, (256, 256), 0) // 64
    lane_head = (lax.broadcasted_iota(jnp.int32, (256, 256), 1) % C) // 32
    own_head = row_head == lane_head
    fold_head = (lax.broadcasted_iota(jnp.int32, (64, 256), 1) % C) // 32

    def per_head(x):
        x = side_by_side(x)
        x = jnp.concatenate([x, x, x, x], axis=0)
        return jnp.where(own_head, x, jnp.zeros_like(x))

    def per_window(x):
        none = jnp.zeros((64, C), x.dtype)
        top = jnp.concatenate([x[:64], none], axis=1)
        low = jnp.concatenate([none, x[64:]], axis=1)
        return jnp.concatenate([top, low], axis=0)

    def fold(x):
        total = x[0:64]
        for h in range(1, HEADS):
            total = jnp.where(fold_head == h, x[h * 64 : (h + 1) * 64], total)
        return stacked(total)

    def windows(src, r0, width, first):
        parts = []
        for c in range(2):
            for il in range(2):
                at = pl.ds(c * (width // 2) + il * 16 + first + r0, 32, stride=width)
                parts.append(src[at, :])
        return jnp.concatenate(parts, axis=0)

    def put(dst, r0, width, first, x):
        for c in range(2):
            for il in range(2):
                at = pl.ds(c * (width // 2) + il * 16 + first + r0, 32, stride=width)
                k = 2 * c + il
                dst[at, :] = x[k * 32 : (k + 1) * 32]

    def pairs(i, carry):
        each = range(PAIRS)
        r0s = [i * PAIRS + p for p in each]
        ms = [windows(mid, r0, 64, 0) for r0 in r0s]
        cts = [windows(cot, r0, 64, 0) for r0 in r0s]
        ctbs = [ct.astype(bf16) for ct in cts]
        scales = [normalise(m) for m in ms]
        normed = [(unit * gain).astype(bf16) for _, unit in scales]
        mixture = [dot(n, wq_ref[...]) for n in normed]
        ga = [dot(ct, wo_ref[...], NT).astype(bf16) for ct in ctbs]
        qd = [per_window((x[:, :C] * scale).astype(bf16)) for x in mixture]
        k4 = [per_head(x[:, C : 2 * C].astype(bf16)) for x in mixture]
        v4 = [per_head(x[:, 2 * C :].astype(bf16)) for x in mixture]
        gd = [per_window(x) for x in ga]
        scores = [dot(k4[p], qd[p], NT) for p in each]
        gp = [dot(v4[p], gd[p], NT).reshape(HEADS, 64, 128) for p in each]
        scores = [(x + bias_ref[...]).reshape(HEADS, 64, 128) for x in scores]
        weights = [jnp.exp(x - jnp.max(x, axis=1, keepdims=True)) for x in scores]
        prob = [x * (1.0 / jnp.sum(x, axis=1, keepdims=True)) for x in weights]
        rounded = [x.reshape(256, 128).astype(bf16) for x in prob]
        att = [diagonal(dot(rounded[p], v4[p], TN)).astype(bf16) for p in each]
        gv = [fold(dot(rounded[p], gd[p])) for p in each]
        gs = [
            prob[p] * (gp[p] - jnp.sum(prob[p] * gp[p], axis=1, keepdims=True)) for p in each
        ]
        gs = [x.reshape(256, 128) for x in gs]
        total = gs[0]
        for x in gs[1:]:
            total = total + x
        ds_ref[...] += total
        gr = [x.astype(bf16) for x in gs]
        gk = [fold(dot(gr[p], qd[p])) for p in each]
        gq = [diagonal(dot(gr[p], k4[p], TN)) * scale for p in each]
        gx = [jnp.concatenate([gq[p], gk[p], gv[p]], axis=1).astype(bf16) for p in each]
        gn = [dot(x, wq_ref[...], NT).astype(bf16).astype(f32) for x in gx]
        mixed = [dot(x, wo_ref[...]) for x in att]
        for p in each:
            at = pl.ds(pl.multiple_of(r0s[p] * 128, 128), 128)
            inverse, unit = scales[p]
            scaled = gn[p] * gain
            mean = jnp.mean(scaled * unit, axis=-1, keepdims=True)
            put(grad, r0s[p], 80, 1, cts[p] + inverse * (scaled - unit * mean))
            put(out, r0s[p], 64, 0, ms[p] + mixed[p])
            norms[at, :] = normed[p]
            atts[at, :] = att[p]
            cots[at, :] = ctbs[p]
            mixes[at, :] = gx[p]
        return carry

    lax.fori_loop(0, 16 // PAIRS, pairs, 0)
    for c in range(2):
        low = grad[pl.ds(c * 40 + 32, 24, stride=80), :]
        high = grad[pl.ds(c * 40 + 1 + 8 * 80, 24, stride=80), :]
        grad[pl.ds(c * 40 + 8 * 80, 24, stride=80), :] = low
        grad[pl.ds(c * 40 + 33, 24, stride=80), :] = high
    back_ref[:, 0:80, :] = grad[...].astype(bf16).reshape(32, 80, C)
    back_ref[:, 80:144, :] = out[...].astype(bf16).reshape(32, 64, C)
    gb_ref[...] = table_sums(ds_ref)
    for k in range(3):
        gq_ref[k * C : (k + 1) * C, :] = dot(norms[...], mixes[:, k * C : (k + 1) * C], TN)
    go_ref[...] = dot(atts[...], cots[...], TN)


def table_sums(ds_ref):
    at = lax.broadcasted_iota(jnp.int32, (128, 128), 0) % 64
    lane = lax.broadcasted_iota(jnp.int32, (128, 128), 1)
    same_row = 2 * (at % 32 // 8) + at // 32 == lane // 16
    total = jnp.zeros((32, 128), f32)
    for col in range(8):
        place = same_row & (at % 8 - col + 7 == lane % 16)
        place = jnp.where(place, 1.0, 0.0).astype(bf16)
        part = ds_ref[pl.ds(col, 32, stride=8), :]
        high = part.astype(bf16)
        rest = part - high.astype(f32)
        total = total + dot(high, place) + dot(rest.astype(bf16), place)
    rows = []
    for h in range(HEADS):
        row_sum = None
        for k in range(8):
            shift = 16 * (7 - (2 * (k % 4) + k // 4))
            part = total[8 * h + k : 8 * h + k + 1]
            none = jnp.zeros((1, 128), f32)
            part = jnp.concatenate([part, none], axis=1)
            part = pltpu.roll(part, shift, 1) if shift else part
            row_sum = part if row_sum is None else row_sum + part
        rows.append(row_sum)
    return jnp.concatenate(rows + [jnp.zeros((4, 256), f32)], axis=0)


def attend(x, gain, wq, wo, bias):
    tokens = RD * CD
    return pl.pallas_call(
        attend_kernel,
        out_shape=[
            jax.ShapeDtypeStruct((32, 144, C), bf16),
            jax.ShapeDtypeStruct((3 * C, C), f32),
            jax.ShapeDtypeStruct((C, C), f32),
            jax.ShapeDtypeStruct((8, 256), f32),
        ],
        scratch_shapes=[
            pltpu.VMEM((tokens, C), f32),
            pltpu.VMEM((tokens, C), f32),
            pltpu.VMEM((tokens, C), f32),
            pltpu.VMEM((32 * 80, C), f32),
            pltpu.VMEM((tokens, C), bf16),
            pltpu.VMEM((tokens, C), bf16),
            pltpu.VMEM((tokens, C), bf16),
            pltpu.VMEM((tokens, 3 * C), bf16),
            pltpu.VMEM((256, 128), f32),
            pltpu.VMEM((C, 3 * C), bf16),
            pltpu.VMEM((C, C), bf16),
        ],
        compiler_params=pltpu.CompilerParams(vmem_limit_bytes=VMEM_LIMIT),
        cost_estimate=pl.CostEstimate(
            flops=40 * tokens * C * C, bytes_accessed=tokens * 8 * C, transcendentals=tokens * 256
        ),
        name="attend",
    )(x, gain, wq, wo, bias)


def project_grad_kernel(g_ref, w2_ref, d_ref, s_ref, b_ref, gp_ref, gm_ref, cols):
    gp_ref[...] = jnp.zeros(gp_ref.shape, f32)
    w2 = w2_ref[...].astype(bf16)
    cols[...] = g_ref[:, 0:80, :].reshape(CD * 40, C).astype(f32)

    def rows(first, count):
        parts = [cols[pl.ds(first + k, CD, stride=40), :] for k in range(count)]
        return jnp.concatenate(parts, axis=0).astype(bf16)

    def before(g, at):
        for k in range(GROUPS):
            wide = dot(g, w2[lane_group(k)], NT)
            wide = wide * s_ref[at, lane_group(k)].astype(f32)
            b_ref[at, lane_group(k)] = wide.astype(bf16)

    def edge(row):
        before(rows(row, 1), pl.ds(row * CD, CD))

    edge(0)
    edge(RD + 1)

    def block(i, carry):
        four = rows_of(i, 4 * CD)
        ring = pl.ds(pl.multiple_of(i * 4 * CD + CD, CD), 4 * CD)
        g = rows(i * 4 + 1, 4)
        gm_ref[four, :] = g
        before(g, ring)
        for k in range(GROUPS):
            gp_ref[lane_group(k), :] += dot(g, d_ref[four, lane_group(k)], TN)
        return carry

    lax.fori_loop(0, RD // 4, block, 0)


def project_grad(gm, w2, depthed, slope):
    tokens = RD * CD
    ring = tokens + 2 * CD
    return pl.pallas_call(
        project_grad_kernel,
        out_shape=[
            jax.ShapeDtypeStruct((ring, E), bf16),
            jax.ShapeDtypeStruct((E, C), f32),
            jax.ShapeDtypeStruct((tokens, C), bf16),
        ],
        scratch_shapes=[pltpu.VMEM((CD * 40, C), f32)],
        compiler_params=pltpu.CompilerParams(vmem_limit_bytes=VMEM_LIMIT),
        cost_estimate=pl.CostEstimate(
            flops=4 * tokens * C * E, bytes_accessed=tokens * (6 * E + 4 * C), transcendentals=0
        ),
        name="project_grad",
    )(gm, w2, depthed, slope)


def depth_grad_kernel(
    b_ref,
    strip_ref,
    ss_ref,
    w2_ref,
    dw_ref,
    e_ref,
    s_ref,
    n_ref,
    gp_ref,
    gq_ref,
    go_ref,
    gb_ref,
    x_ref,
    pack_ref,
    ext,
    sums,
    total,
):
    w2 = w2_ref[...].astype(bf16)
    strip = strip_ref[...].reshape(2 * 48, C)
    for g in range(GROUPS):
        wide = dot(strip, w2[lane_group(g)], NT).reshape(2, 48, LANES)
        wide = (wide * ss_ref[:, :, lane_group(g)].astype(f32)).astype(bf16).astype(f32)
        for row in range(RD + 2):
            ext[g, row, 15:16, :] = wide[0, row : row + 1]
            ext[g, row, 16 + CD : 17 + CD, :] = wide[1, row : row + 1]

    def fill(first, count):
        for k in range(count):
            for g in range(GROUPS):
                part = b_ref[first + k, :, lane_group(g)]
                ext[g, first + k, 16 : 16 + CD, :] = part.astype(f32)

    fill(0, 2)
    sums[...] = jnp.zeros(sums.shape, f32)
    total[...] = jnp.zeros(total.shape, f32)

    def block(i, carry):
        fill(i * 4 + 2, 4)
        for k in range(4):
            row = i * 4 + k
            at = pl.ds(pl.multiple_of(row * CD, CD), CD)
            for g in range(GROUPS):
                own = e_ref[at, lane_group(g)].astype(f32)
                running = None
                for t in range(9):
                    window = ext[g, row + t // 3, 15 + t % 3 : 15 + t % 3 + CD, :]
                    term = dw_ref[8 - t : 9 - t, lane_group(g)] * window
                    running = term if running is None else running + term
                    sums[g, 8 - t] += jnp.sum((own * window).reshape(CD // 8, 8, LANES), axis=0)
                wide = running * s_ref[at, lane_group(g)].astype(f32)
                x_ref[at, lane_group(g)] = wide.astype(bf16)
        four = pl.ds(pl.multiple_of(i * 4 * CD, 4 * CD), 4 * CD)
        normed = n_ref[four, :]
        for g in range(GROUPS):
            total[lane_group(g), :] += dot(normed, x_ref[four, lane_group(g)], TN)
        return carry

    lax.fori_loop(0, RD // 4, block, 0)
    pack_ref[ROW_EXPAND : ROW_EXPAND + E, :] = total[...].astype(bf16)
    pack_ref[ROW_PROJECT : ROW_PROJECT + E, :] = gp_ref[...].astype(bf16)
    pack_ref[ROW_QKV : ROW_QKV + 3 * C, :] = gq_ref[...].astype(bf16)
    pack_ref[ROW_OUT : ROW_OUT + C, :] = go_ref[...].astype(bf16)
    for g in range(GROUPS):
        kernel_sums = jnp.sum(sums[g], axis=1)
        kernel_sums = jnp.concatenate([kernel_sums, jnp.zeros((7, LANES), f32)], axis=0)
        pack_ref[ROW_KERNEL + 16 * g : ROW_KERNEL + 16 * g + 16, :] = kernel_sums.astype(bf16)
    table = jnp.concatenate([gb_ref[:, :LANES], gb_ref[:, LANES:]], axis=0)
    pack_ref[ROW_BIAS : ROW_BIAS + 16, :] = table.astype(bf16)
    pack_ref[ROWS_USED:PACK_ROWS, :] = jnp.zeros((PACK_ROWS - ROWS_USED, C), bf16)


def depth_grad(before, strip, ss, w2, taps, expanded, slope, normed, gp, gq, go, gb):
    tokens = RD * CD
    return pl.pallas_call(
        depth_grad_kernel,
        out_shape=[
            jax.ShapeDtypeStruct((tokens, E), bf16),
            jax.ShapeDtypeStruct((PACK_ROWS, C), bf16),
        ],
        scratch_shapes=[
            pltpu.VMEM((GROUPS, RD + 2, 96, LANES), f32),
            pltpu.VMEM((GROUPS, 9, 8, LANES), f32),
            pltpu.VMEM((E, C), f32),
        ],
        compiler_params=pltpu.CompilerParams(vmem_limit_bytes=VMEM_LIMIT),
        cost_estimate=pl.CostEstimate(
            flops=2 * tokens * C * E + 60 * tokens * E,
            bytes_accessed=tokens * (8 * E + 4 * C),
            transcendentals=0,
        ),
        name="depth_grad",
    )(
        before.reshape(RD + 2, CD, E), strip, ss, w2, taps, expanded, slope, normed, gp, gq, go, gb
    )


def image_grad_kernel(g_ref, w_ref, gain_ref, x_ref, m_ref, o_ref):
    w = w_ref[...].astype(bf16)

    def step(i, carry):
        at = pl.ds(pl.multiple_of(i * 256, 256), 256)
        scaled = dot(g_ref[at, :], w, NT) * gain_ref[...]
        inverse, unit = normalise(x_ref[at, :].astype(f32))
        mean = jnp.mean(scaled * unit, axis=-1, keepdims=True)
        o_ref[at, :] = (m_ref[at, :].astype(f32) + inverse * (scaled - unit * mean)).astype(bf16)
        return carry

    lax.fori_loop(0, x_ref.shape[0] // 256, step, 0)


def image_grad(g, w, gain, x, gm):
    tokens = x.shape[0]
    return pl.pallas_call(
        image_grad_kernel,
        out_shape=jax.ShapeDtypeStruct((tokens, C), bf16),
        compiler_params=pltpu.CompilerParams(vmem_limit_bytes=VMEM_LIMIT),
        cost_estimate=pl.CostEstimate(
            flops=2 * tokens * C * E, bytes_accessed=tokens * (2 * E + 6 * C), transcendentals=0
        ),
        name="image_grad",
    )(g, w, gain, x, gm)


def sum_parts_kernel(factor, x_hbm, o_hbm, x_ref, o_ref, xs, outs):
    x_in = Blocks(x_hbm, x_ref, xs, 32)
    x_in.start_all()
    total = jnp.zeros(x_ref.shape[1:], f32)
    for i in range(4):
        x_in.copy(i).wait()
        for k in range(32):
            total = total + x_ref[32 * i + k].astype(f32)
    total = (total * factor).astype(bf16)
    for k in range(16):
        o_ref[k] = total
    spread = [(o_ref, o_hbm.at[pl.ds(16 * k, 16)]) for k in range(8)]
    spread = copies(spread, outs)
    for copy in spread:
        copy.start()
    for copy in spread:
        copy.wait()


def sum_parts(x, factor):
    return pl.pallas_call(
        lambda *refs: sum_parts_kernel(factor, *refs),
        out_shape=jax.ShapeDtypeStruct(x.shape, bf16),
        in_specs=[HBM],
        out_specs=HBM,
        scratch_shapes=[
            pltpu.VMEM(x.shape, bf16),
            pltpu.VMEM((16,) + x.shape[1:], bf16),
            pltpu.SemaphoreType.DMA((4,)),
            pltpu.SemaphoreType.DMA((8,)),
        ],
        compiler_params=pltpu.CompilerParams(vmem_limit_bytes=VMEM_LIMIT),
        cost_estimate=pl.CostEstimate(
            flops=2 * x.size, bytes_accessed=4 * x.size, transcendentals=0
        ),
        name="sum_parts",
    )(x)


def column_sums(x):
    line = jnp.sum(x, axis=1, keepdims=True)
    return jnp.broadcast_to(line, (C, C)).T[0:1]


def unpack_kernel(
    p_ref, w1_ref, wq_ref, gain1_ref, gain2_ref, g1_ref, ex_ref, k_ref, pr_ref, g2_ref, qk_ref,
    o_ref, b_ref
):
    first = jnp.zeros((C, C), f32)
    second = jnp.zeros((C, C), f32)
    for g in range(GROUPS):
        part = p_ref[ROW_EXPAND + g * C : ROW_EXPAND + (g + 1) * C, :].astype(f32)
        ex_ref[:, lane_group(g)] = part
        first = first + part * w1_ref[:, lane_group(g)].astype(bf16).astype(f32)
        part = p_ref[ROW_PROJECT + g * C : ROW_PROJECT + (g + 1) * C, :].astype(f32)
        pr_ref[g * C : (g + 1) * C, :] = part.T
        part = p_ref[ROW_KERNEL + g * 16 : ROW_KERNEL + (g + 1) * 16, :].astype(f32)
        k_ref[:, lane_group(g)] = part[0:9]
    for k in range(3):
        part = p_ref[ROW_QKV + k * C : ROW_QKV + (k + 1) * C, :].astype(f32)
        qk_ref[:, lane_group(k)] = part
        second = second + part * wq_ref[:, lane_group(k)].astype(bf16).astype(f32)
    g1_ref[...] = column_sums(first) / gain1_ref[...]
    g2_ref[...] = column_sums(second) / gain2_ref[...]
    o_ref[...] = p_ref[ROW_OUT : ROW_OUT + C, :].astype(f32)
    part = p_ref[ROW_BIAS : ROW_BIAS + 16, :].astype(f32)
    table = jnp.concatenate([part[0:4], part[8:12]], axis=1)
    b_ref[...] = jnp.concatenate([table[:, 16 * k : 16 * k + 15] for k in range(15)], axis=1)


def unpack(pack, w1, wq, gain1, gain2):
    return pl.pallas_call(
        unpack_kernel,
        out_shape=[
            jax.ShapeDtypeStruct((1, C), f32),
            jax.ShapeDtypeStruct((C, E), f32),
            jax.ShapeDtypeStruct((9, E), f32),
            jax.ShapeDtypeStruct((E, C), f32),
            jax.ShapeDtypeStruct((1, C), f32),
            jax.ShapeDtypeStruct((C, 3 * C), f32),
            jax.ShapeDtypeStruct((C, C), f32),
            jax.ShapeDtypeStruct((HEADS, 225), f32),
        ],
        compiler_params=pltpu.CompilerParams(vmem_limit_bytes=VMEM_LIMIT),
        cost_estimate=pl.CostEstimate(
            flops=4 * pack.size, bytes_accessed=6 * pack.size, transcendentals=0
        ),
        name="unpack",
    )(pack, w1, wq, gain1, gain2)


def pair_onehot():
    place = np.arange(64)
    row = 2 * ((place % 32) // 8) + place // 32
    col = place % 8
    first, second = place[None, :], place[:, None]
    index = 15 * (row[first] - row[second] + 7) + col[first] - col[second] + 7
    index = jnp.asarray(np.concatenate([index, index], axis=1), jnp.int32)
    return (index[:, :, None] == jnp.arange(225, dtype=jnp.int32)).astype(f32)


def swap_ends(low, high, axis):
    count = lax.axis_size(axis)
    odd = lax.axis_index(axis) % 2 == 1
    pairs = [(i, i ^ 1) for i in range(count)]
    others = [(i, ((i - 1) ^ 1) + 1) for i in range(1, count - 1)]
    first = lax.ppermute(jnp.where(odd, low, high), axis, pairs)
    second = lax.ppermute(jnp.where(odd, high, low), axis, others)
    return jnp.where(odd, first, second), jnp.where(odd, second, first)


def per_device(
    image,
    cotangent,
    norm1_gain,
    w_expand,
    dw_kernel,
    w_project,
    norm2_gain,
    w_qkv,
    w_out,
    bias_table,
):
    factor = 1.0 / math.sqrt(RD * CD * 128)
    w1, w2, wq, wo = w_expand, w_project, w_qkv, w_out
    gain1 = norm1_gain.reshape(1, C)
    gain2 = norm2_gain.reshape(1, C)
    onehot = pair_onehot()
    bias = jnp.einsum("hq,jlq->hjl", bias_table, onehot, precision=lax.Precision.HIGHEST)
    bias = bias.reshape(HEADS * 64, 128)

    tokens = image.reshape(RD * CD, C)
    above, below = swap_ends(tokens[: 2 * CD], tokens[(RD - 2) * CD :], "rows")
    above = above.reshape(2, CD, C)
    below = below.reshape(2, CD, C)
    left = jnp.concatenate([above[:, :2], image[:, :2], below[:, :2]], axis=0)
    right = jnp.concatenate([above[:, -2:], image[:, -2:], below[:, -2:]], axis=0)
    left = left.transpose(1, 0, 2)
    right = right.transpose(1, 0, 2)
    before_left, after_right = swap_ends(left, right, COLS)
    expanded, slope1, normed1 = expand(tokens, gain1, w1)
    halo = jnp.concatenate([above, below], axis=0)
    strip = jnp.concatenate([before_left, left[:1], right[1:], after_right], axis=0)
    strip = jnp.pad(strip, ((0, 0), (0, 12), (0, 0)))
    send, depthed, slope2, slope2_strip = depth(
        expanded, tokens, to_columns(cotangent), halo, strip, gain1, w1, dw_kernel, w2
    )
    send, bias = lax.optimization_barrier((send, bias))
    windows = lax.all_to_all(send, PLANE, 0, 0, tiled=True)
    back, grad_qkv, grad_out, grad_bias = attend(windows, gain2, wq, wo, bias)
    back = lax.all_to_all(back, PLANE, 0, 0, tiled=True)
    grad_left, grad_right = swap_ends(back[0, :40], back[31, 40:80], COLS)
    before, grad_project, grad_middle = project_grad(back, w2, depthed, slope2)
    grad_strip = jnp.pad(jnp.stack([grad_left, grad_right]), ((0, 0), (0, 8), (0, 0)))
    grad_wide, pack = depth_grad(
        before, grad_strip, slope2_strip, w2, dw_kernel, expanded, slope1, normed1,
        grad_project, grad_qkv, grad_out, grad_bias,
    )
    parts = lax.all_to_all(pack.reshape(128, 16, C), ALL, 0, 0, tiled=True)
    grad_image = image_grad(grad_wide, w1, gain1, tokens, grad_middle)
    parts, grad_image = lax.optimization_barrier((parts, grad_image))
    block_out = from_columns(back)
    whole = lax.all_to_all(sum_parts(parts, factor), ALL, 0, 0, tiled=True)
    g1, ge, gk, gp, g2, gq, go, gb = unpack(whole.reshape(PACK_ROWS, C), w1, wq, gain1, gain2)
    return (
        block_out,
        grad_image.reshape(RD, CD, C),
        g1.reshape(C),
        ge,
        gk,
        gp,
        g2.reshape(C),
        gq,
        go,
        gb,
    )


def solution(mesh):
    mesh = Mesh(mesh.devices.reshape(4, 8, 4), ALL)
    tiles = P("rows", COLS, None)
    return jax.shard_map(
        per_device,
        mesh=mesh,
        in_specs=(tiles, tiles) + (P(),) * 8,
        out_specs=(tiles, tiles) + (P(),) * 8,
        check_vma=False,
    )
```

```python
import math

import jax
import jax.numpy as jnp
from jax import lax
from jax.experimental import pallas as pl
from jax.experimental.pallas import tpu as pltpu
from jax.sharding import Mesh
from jax.sharding import PartitionSpec as P

GRID = 8
C = 128
E = 512
HEADS = 4
RD = 32
CD = 64
LANES = 128
GROUPS = E // LANES
epsilon = 1e-06
gelu_coef = math.sqrt(2.0 / math.pi)
bf16 = jnp.bfloat16
f32 = jnp.float32
VMEM_LIMIT = 24 * 1024 * 1024

PLANE = ("rows", "group")
COLS = ("group", "plane")
ALL = ("rows", "group", "plane")

ROW_EXPAND = 0
ROW_PROJECT = 512
ROW_QKV = 1024
ROW_OUT = 1408
ROW_KERNEL = 1536
ROW_BIAS = 1600
ROWS_USED = 1616
PACK_ROWS = 2048

PAIRS = 8

HBM = pl.BlockSpec(memory_space=pltpu.HBM)
ANY = pl.BlockSpec()
NT = (((1,), (1,)), ((), ()))
TN = (((0,), (0,)), ((), ()))


def dot(a, b, dims=(((1,), (0,)), ((), ()))):
    return lax.dot_general(a, b, dims, preferred_element_type=f32)


def gelu_value(t):
    t2 = t * t
    u = jnp.tanh(t * (t2 * (0.044715 * gelu_coef) + gelu_coef))
    return t * (0.5 * u + 0.5)


def gelu_pair(t):
    t2 = t * t
    u = jnp.tanh(t * (t2 * (0.044715 * gelu_coef) + gelu_coef))
    h = 0.5 * u + 0.5
    value = t * h
    slope = h + value * (1.0 - h) * (t2 * (2.0 * 0.134145 * gelu_coef) + 2.0 * gelu_coef)
    return value, slope


def normalise(v):
    inverse = lax.rsqrt(jnp.mean(v * v, axis=-1, keepdims=True) + epsilon)
    return inverse, v * inverse


def rows_of(i, count):
    return pl.ds(pl.multiple_of(i * count, count), count)


def copies(pairs, sems):
    return [pltpu.make_async_copy(a, b, sems.at[k]) for k, (a, b) in enumerate(pairs)]


class Blocks:
    def __init__(self, src, dst, sems, count):
        self.src, self.dst, self.sems, self.count = src, dst, sems, count
        self.steps = src.shape[0] // count

    def copy(self, i):
        at = rows_of(i, self.count) if not isinstance(i, int) else pl.ds(i * self.count, self.count)
        return pltpu.make_async_copy(self.src.at[at], self.dst.at[at], self.sems.at[i])

    def start_all(self):
        for i in range(self.steps):
            self.copy(i).start()

    def wait_all(self):
        for i in range(self.steps):
            self.copy(i).wait()


def lane_group(g):
    return slice(g * LANES, (g + 1) * LANES)


def to_columns_kernel(x_ref, o_ref, rows):
    rows[...] = x_ref[...].reshape(RD * CD, C).astype(f32)
    for col in range(CD):
        part = rows[pl.ds(col, RD, stride=CD), :]
        o_ref[col // 2, (col % 2) * RD : (col % 2 + 1) * RD, :] = part.astype(bf16)


def to_columns(x):
    return pl.pallas_call(
        to_columns_kernel,
        out_shape=jax.ShapeDtypeStruct((CD // 2, 2 * RD, C), bf16),
        scratch_shapes=[pltpu.VMEM((RD * CD, C), f32)],
        compiler_params=pltpu.CompilerParams(vmem_limit_bytes=VMEM_LIMIT),
        cost_estimate=pl.CostEstimate(flops=0, bytes_accessed=4 * RD * CD * C, transcendentals=0),
        name="to_columns",
    )(x)


def from_columns_kernel(x_ref, o_ref, cols):
    cols[...] = x_ref[:, 80:144, :].reshape(RD * CD, C).astype(f32)
    for row in range(RD):
        o_ref[row, :, :] = cols[pl.ds(row, CD, stride=RD), :].astype(bf16)


def from_columns(x):
    return pl.pallas_call(
        from_columns_kernel,
        out_shape=jax.ShapeDtypeStruct((RD, CD, C), bf16),
        scratch_shapes=[pltpu.VMEM((RD * CD, C), f32)],
        compiler_params=pltpu.CompilerParams(vmem_limit_bytes=VMEM_LIMIT),
        cost_estimate=pl.CostEstimate(flops=0, bytes_accessed=4 * RD * CD * C, transcendentals=0),
        name="from_columns",
    )(x)


def expand_kernel(x_ref, gain_ref, w_ref, e_ref, s_ref, n_ref):
    w = w_ref[...].astype(bf16)

    def step(i, carry):
        at = pl.ds(pl.multiple_of(i * 256, 256), 256)
        normed = (normalise(x_ref[at, :].astype(f32))[1] * gain_ref[...]).astype(bf16)
        n_ref[at, :] = normed
        for g in range(GROUPS):
            value, slope = gelu_pair(dot(normed, w[:, lane_group(g)]))
            e_ref[at, lane_group(g)] = value.astype(bf16)
            s_ref[at, lane_group(g)] = slope.astype(bf16)
        return carry

    lax.fori_loop(0, x_ref.shape[0] // 256, step, 0)


def expand(x, gain, w):
    tokens = x.shape[0]
    return pl.pallas_call(
        expand_kernel,
        out_shape=[
            jax.ShapeDtypeStruct((tokens, E), bf16),
            jax.ShapeDtypeStruct((tokens, E), bf16),
            jax.ShapeDtypeStruct((tokens, C), bf16),
        ],
        compiler_params=pltpu.CompilerParams(vmem_limit_bytes=VMEM_LIMIT),
        cost_estimate=pl.CostEstimate(
            flops=2 * tokens * C * E + 20 * tokens * E,
            bytes_accessed=tokens * (4 * E + 4 * C),
            transcendentals=tokens * E,
        ),
        name="expand",
    )(x, gain, w)


def conv_row(src, taps, g, row):
    total = None
    for a in range(3):
        for b in range(3):
            term = taps[3 * a + b] * src[g, row + a, 15 + b : 15 + b + CD, :]
            total = term if total is None else total + term
    return total


def depth_kernel(
    e_ref,
    x_ref,
    c_ref,
    halo_ref,
    strip_ref,
    gain_ref,
    w1_ref,
    dw_ref,
    w2f_ref,
    send_ref,
    d_ref,
    s_ref,
    ss_ref,
    ext,
    side,
    mid,
    w2_ref,
):
    w2_ref[...] = w2f_ref[...].astype(bf16)
    send_ref[:, 64:128, :] = c_ref[...]
    gain = gain_ref[...]
    halo = normalise(halo_ref[...].reshape(4 * CD, C).astype(f32))[1]
    halo = (halo * gain).astype(bf16)
    strip = normalise(strip_ref[...].reshape(6 * 48, C).astype(f32))[1]
    strip = (strip * gain).astype(bf16)
    for g in range(GROUPS):
        weight = w1_ref[:, lane_group(g)].astype(bf16)
        value = gelu_value(dot(halo, weight)).astype(bf16).astype(f32).reshape(4, CD, C)
        for k, row in enumerate((0, 1, RD + 2, RD + 3)):
            ext[g, row, 16 : 16 + CD, :] = value[k]
        value = gelu_value(dot(strip, weight)).astype(bf16).astype(f32).reshape(6, 48, C)
        side[g, :, 0:48, :] = value
        side[g, :, 48:56, :] = jnp.zeros((6, 8, C), f32)
        for row in range(RD + 4):
            ext[g, row, 15:16, :] = value[1, row : row + 1]
            ext[g, row, 16 + CD : 17 + CD, :] = value[4, row : row + 1]

    def fill(i):
        for k in range(4):
            row = i * 4 + k
            for g in range(GROUPS):
                ext[g, row + 2, 16 : 16 + CD, :] = e_ref[row, :, lane_group(g)].astype(f32)

    def taps_of(g):
        return [dw_ref[t : t + 1, lane_group(g)] for t in range(9)]

    fill(0)

    def block(i, carry):
        @pl.when(i < RD // 4 - 1)
        def _():
            fill(i + 1)

        for k in range(4):
            row = i * 4 + k
            at = pl.ds(pl.multiple_of(row * CD, CD), CD)
            ring = pl.ds(pl.multiple_of(row * CD + CD, CD), CD)
            for g in range(GROUPS):
                value, slope = gelu_pair(conv_row(ext, taps_of(g), g, row + 1))
                d_ref[at, lane_group(g)] = value.astype(bf16)
                s_ref[ring, lane_group(g)] = slope.astype(bf16)
        four = pl.ds(pl.multiple_of(i * 4 * CD, 4 * CD), 4 * CD)
        mid[four, :] = x_ref[four, :].astype(f32) + dot(d_ref[four, :], w2_ref[...])
        return carry

    lax.fori_loop(0, RD // 4, block, 0)
    for col in range(CD):
        part = mid[pl.ds(col, RD, stride=CD), :]
        send_ref[col // 2, (col % 2) * RD : (col % 2 + 1) * RD, :] = part.astype(bf16)
    for g in range(GROUPS):
        taps = taps_of(g)
        for row in (0, RD + 1):
            slope = gelu_pair(conv_row(ext, taps, g, row))[1]
            s_ref[row * CD : (row + 1) * CD, lane_group(g)] = slope.astype(bf16)
        for end in range(2):
            total = None
            for a in range(3):
                for b in range(3):
                    term = taps[3 * a + b] * side[g, 3 * end + b, a : a + 48, :]
                    total = term if total is None else total + term
            ss_ref[end, :, lane_group(g)] = gelu_pair(total)[1].astype(bf16)


def depth(expanded, x, cot, halo, strip, gain, w1, taps, w2):
    tokens = RD * CD
    return pl.pallas_call(
        depth_kernel,
        out_shape=[
            jax.ShapeDtypeStruct((CD // 2, 4 * RD, C), bf16),
            jax.ShapeDtypeStruct((tokens, E), bf16),
            jax.ShapeDtypeStruct((tokens + 2 * CD, E), bf16),
            jax.ShapeDtypeStruct((2, 48, E), bf16),
        ],
        scratch_shapes=[
            pltpu.VMEM((GROUPS, RD + 4, 96, LANES), f32),
            pltpu.VMEM((GROUPS, 6, 56, LANES), f32),
            pltpu.VMEM((tokens, C), f32),
            pltpu.VMEM((E, C), bf16),
        ],
        compiler_params=pltpu.CompilerParams(vmem_limit_bytes=VMEM_LIMIT),
        cost_estimate=pl.CostEstimate(
            flops=2 * tokens * C * E + 40 * tokens * E,
            bytes_accessed=tokens * (6 * E + 4 * C),
            transcendentals=tokens * E,
        ),
        name="depth",
    )(expanded.reshape(RD, CD, E), x, cot, halo, strip, gain, w1, taps, w2)


def side_by_side(x):
    return jnp.concatenate([x[:64], x[64:]], axis=1)


def stacked(x):
    return jnp.concatenate([x[:, :C], x[:, C:]], axis=0)


def diagonal(x):
    return jnp.concatenate([x[:64, :C], x[64:, C:]], axis=0)


def attend_kernel(
    x_ref,
    gain_ref,
    wqf_ref,
    wof_ref,
    table_ref,
    back_ref,
    gq_ref,
    go_ref,
    gb_ref,
    mid,
    cot,
    out,
    grad,
    norms,
    atts,
    cots,
    mixes,
    ds_ref,
    wq_ref,
    wo_ref,
    bias_ref,
):
    spread_table(table_ref, bias_ref)
    grad[...] = jnp.zeros(grad.shape, f32)
    ds_ref[...] = jnp.zeros(ds_ref.shape, f32)
    wq_ref[...] = wqf_ref[...].astype(bf16)
    wo_ref[...] = wof_ref[...].astype(bf16)
    mid[...] = x_ref[:, 0:64, :].reshape(RD * CD, C).astype(f32)
    cot[...] = x_ref[:, 64:128, :].reshape(RD * CD, C).astype(f32)
    gain = gain_ref[...]
    scale = 32**-0.5
    row_head = lax.broadcasted_iota(jnp.int32, (256, 256), 0) // 64
    lane_head = (lax.broadcasted_iota(jnp.int32, (256, 256), 1) % C) // 32
    own_head = row_head == lane_head
    fold_head = (lax.broadcasted_iota(jnp.int32, (64, 256), 1) % C) // 32

    def per_head(x):
        x = side_by_side(x)
        x = jnp.concatenate([x, x, x, x], axis=0)
        return jnp.where(own_head, x, jnp.zeros_like(x))

    def per_window(x):
        none = jnp.zeros((64, C), x.dtype)
        top = jnp.concatenate([x[:64], none], axis=1)
        low = jnp.concatenate([none, x[64:]], axis=1)
        return jnp.concatenate([top, low], axis=0)

    def fold(x):
        total = x[0:64]
        for h in range(1, HEADS):
            total = jnp.where(fold_head == h, x[h * 64 : (h + 1) * 64], total)
        return stacked(total)

    def windows(src, r0, width, first):
        parts = []
        for c in range(2):
            for il in range(2):
                at = pl.ds(c * (width // 2) + il * 16 + first + r0, 32, stride=width)
                parts.append(src[at, :])
        return jnp.concatenate(parts, axis=0)

    def put(dst, r0, width, first, x):
        for c in range(2):
            for il in range(2):
                at = pl.ds(c * (width // 2) + il * 16 + first + r0, 32, stride=width)
                k = 2 * c + il
                dst[at, :] = x[k * 32 : (k + 1) * 32]

    def pairs(i, carry):
        each = range(PAIRS)
        r0s = [i * PAIRS + p for p in each]
        ms = [windows(mid, r0, 64, 0) for r0 in r0s]
        cts = [windows(cot, r0, 64, 0) for r0 in r0s]
        ctbs = [ct.astype(bf16) for ct in cts]
        scales = [normalise(m) for m in ms]
        normed = [(unit * gain).astype(bf16) for _, unit in scales]
        mixture = [dot(n, wq_ref[...]) for n in normed]
        ga = [dot(ct, wo_ref[...], NT).astype(bf16) for ct in ctbs]
        qd = [per_window((x[:, :C] * scale).astype(bf16)) for x in mixture]
        k4 = [per_head(x[:, C : 2 * C].astype(bf16)) for x in mixture]
        v4 = [per_head(x[:, 2 * C :].astype(bf16)) for x in mixture]
        gd = [per_window(x) for x in ga]
        scores = [dot(k4[p], qd[p], NT) for p in each]
        gp = [dot(v4[p], gd[p], NT).reshape(HEADS, 64, 128) for p in each]
        scores = [(x + bias_ref[...]).reshape(HEADS, 64, 128) for x in scores]
        weights = [jnp.exp(x - jnp.max(x, axis=1, keepdims=True)) for x in scores]
        prob = [x * (1.0 / jnp.sum(x, axis=1, keepdims=True)) for x in weights]
        rounded = [x.reshape(256, 128).astype(bf16) for x in prob]
        att = [diagonal(dot(rounded[p], v4[p], TN)).astype(bf16) for p in each]
        gv = [fold(dot(rounded[p], gd[p])) for p in each]
        gs = [
            prob[p] * (gp[p] - jnp.sum(prob[p] * gp[p], axis=1, keepdims=True)) for p in each
        ]
        gs = [x.reshape(256, 128) for x in gs]
        total = gs[0]
        for x in gs[1:]:
            total = total + x
        ds_ref[...] += total
        gr = [x.astype(bf16) for x in gs]
        gk = [fold(dot(gr[p], qd[p])) for p in each]
        gq = [diagonal(dot(gr[p], k4[p], TN)) * scale for p in each]
        gx = [jnp.concatenate([gq[p], gk[p], gv[p]], axis=1).astype(bf16) for p in each]
        gn = [dot(x, wq_ref[...], NT).astype(bf16).astype(f32) for x in gx]
        mixed = [dot(x, wo_ref[...]) for x in att]
        for p in each:
            at = pl.ds(pl.multiple_of(r0s[p] * 128, 128), 128)
            inverse, unit = scales[p]
            scaled = gn[p] * gain
            mean = jnp.mean(scaled * unit, axis=-1, keepdims=True)
            put(grad, r0s[p], 80, 1, cts[p] + inverse * (scaled - unit * mean))
            put(out, r0s[p], 64, 0, ms[p] + mixed[p])
            norms[at, :] = normed[p]
            atts[at, :] = att[p]
            cots[at, :] = ctbs[p]
            mixes[at, :] = gx[p]
        return carry

    lax.fori_loop(0, 16 // PAIRS, pairs, 0)
    for c in range(2):
        low = grad[pl.ds(c * 40 + 32, 24, stride=80), :]
        high = grad[pl.ds(c * 40 + 1 + 8 * 80, 24, stride=80), :]
        grad[pl.ds(c * 40 + 8 * 80, 24, stride=80), :] = low
        grad[pl.ds(c * 40 + 33, 24, stride=80), :] = high
    back_ref[:, 0:80, :] = grad[...].astype(bf16).reshape(32, 80, C)
    back_ref[:, 80:144, :] = out[...].astype(bf16).reshape(32, 64, C)
    gb_ref[...] = table_sums(ds_ref)
    for k in range(3):
        gq_ref[k * C : (k + 1) * C, :] = dot(norms[...], mixes[:, k * C : (k + 1) * C], TN)
    go_ref[...] = dot(atts[...], cots[...], TN)


def place_of(col):
    at = lax.broadcasted_iota(jnp.int32, (128, 128), 0) % 64
    lane = lax.broadcasted_iota(jnp.int32, (128, 128), 1)
    fits = (2 * (at % 32 // 8) + at // 32 == lane // 16) & (at % 8 - col + 7 == lane % 16)
    return jnp.where(fits, 1.0, 0.0).astype(bf16)


def row_of(k):
    return 2 * (k % 4) + k // 4


def spread_table(table_ref, bias_ref):
    none = jnp.zeros((HEADS, 1), f32)
    parts = []
    for k in range(15):
        parts += [table_ref[:, 15 * k : 15 * k + 15], none]
    table = jnp.concatenate(parts + [jnp.zeros((HEADS, 16), f32)], axis=1)
    shifted = [table[:, 16 * (7 - row_of(k)) : 16 * (7 - row_of(k)) + 128] for k in range(8)]
    rows = [shifted[k][h : h + 1] for h in range(HEADS) for k in range(8)]
    rows = jnp.concatenate(rows, axis=0)
    terms = []
    for _ in range(3):
        terms.append(rows.astype(bf16))
        rows = rows - terms[-1].astype(f32)
    terms = jnp.concatenate(terms, axis=0)
    for col in range(8):
        part = dot(terms, place_of(col), NT)
        bias_ref[pl.ds(col, 32, stride=8), :] = part[0:32] + part[32:64] + part[64:96]


def table_sums(ds_ref):
    total = jnp.zeros((32, 128), f32)
    for col in range(8):
        part = ds_ref[pl.ds(col, 32, stride=8), :]
        high = part.astype(bf16)
        rest = (part - high.astype(f32)).astype(bf16)
        both = dot(jnp.concatenate([high, rest], axis=0), place_of(col))
        total = total + both[0:32] + both[32:64]
    rows = []
    for h in range(HEADS):
        row_sum = None
        for k in range(8):
            shift = 16 * (7 - row_of(k))
            part = total[8 * h + k : 8 * h + k + 1]
            none = jnp.zeros((1, 128), f32)
            part = jnp.concatenate([part, none], axis=1)
            part = pltpu.roll(part, shift, 1) if shift else part
            row_sum = part if row_sum is None else row_sum + part
        rows.append(row_sum)
    return jnp.concatenate(rows + [jnp.zeros((4, 256), f32)], axis=0)


def attend(x, gain, wq, wo, table):
    tokens = RD * CD
    return pl.pallas_call(
        attend_kernel,
        out_shape=[
            jax.ShapeDtypeStruct((32, 144, C), bf16),
            jax.ShapeDtypeStruct((3 * C, C), f32),
            jax.ShapeDtypeStruct((C, C), f32),
            jax.ShapeDtypeStruct((8, 256), f32),
        ],
        scratch_shapes=[
            pltpu.VMEM((tokens, C), f32),
            pltpu.VMEM((tokens, C), f32),
            pltpu.VMEM((tokens, C), f32),
            pltpu.VMEM((32 * 80, C), f32),
            pltpu.VMEM((tokens, C), bf16),
            pltpu.VMEM((tokens, C), bf16),
            pltpu.VMEM((tokens, C), bf16),
            pltpu.VMEM((tokens, 3 * C), bf16),
            pltpu.VMEM((256, 128), f32),
            pltpu.VMEM((C, 3 * C), bf16),
            pltpu.VMEM((C, C), bf16),
            pltpu.VMEM((256, 128), f32),
        ],
        compiler_params=pltpu.CompilerParams(vmem_limit_bytes=VMEM_LIMIT),
        cost_estimate=pl.CostEstimate(
            flops=40 * tokens * C * C, bytes_accessed=tokens * 8 * C, transcendentals=tokens * 256
        ),
        name="attend",
    )(x, gain, wq, wo, table)


def project_grad_kernel(g_ref, w2_ref, d_ref, s_ref, b_ref, gp_ref, gm_ref, cols):
    gp_ref[...] = jnp.zeros(gp_ref.shape, f32)
    w2 = w2_ref[...].astype(bf16)
    cols[...] = g_ref[:, 0:80, :].reshape(CD * 40, C).astype(f32)

    def rows(first, count):
        parts = [cols[pl.ds(first + k, CD, stride=40), :] for k in range(count)]
        return jnp.concatenate(parts, axis=0).astype(bf16)

    def before(g, at):
        for k in range(GROUPS):
            wide = dot(g, w2[lane_group(k)], NT)
            wide = wide * s_ref[at, lane_group(k)].astype(f32)
            b_ref[at, lane_group(k)] = wide.astype(bf16)

    def edge(row):
        before(rows(row, 1), pl.ds(row * CD, CD))

    edge(0)
    edge(RD + 1)

    def block(i, carry):
        four = rows_of(i, 4 * CD)
        ring = pl.ds(pl.multiple_of(i * 4 * CD + CD, CD), 4 * CD)
        g = rows(i * 4 + 1, 4)
        gm_ref[four, :] = g
        before(g, ring)
        for k in range(GROUPS):
            gp_ref[lane_group(k), :] += dot(g, d_ref[four, lane_group(k)], TN)
        return carry

    lax.fori_loop(0, RD // 4, block, 0)


def project_grad(gm, w2, depthed, slope):
    tokens = RD * CD
    ring = tokens + 2 * CD
    return pl.pallas_call(
        project_grad_kernel,
        out_shape=[
            jax.ShapeDtypeStruct((ring, E), bf16),
            jax.ShapeDtypeStruct((E, C), f32),
            jax.ShapeDtypeStruct((tokens, C), bf16),
        ],
        scratch_shapes=[pltpu.VMEM((CD * 40, C), f32)],
        compiler_params=pltpu.CompilerParams(vmem_limit_bytes=VMEM_LIMIT),
        cost_estimate=pl.CostEstimate(
            flops=4 * tokens * C * E, bytes_accessed=tokens * (6 * E + 4 * C), transcendentals=0
        ),
        name="project_grad",
    )(gm, w2, depthed, slope)


def depth_grad_kernel(
    b_ref,
    strip_ref,
    ss_ref,
    w2_ref,
    dw_ref,
    e_ref,
    s_ref,
    n_ref,
    gp_ref,
    gq_ref,
    go_ref,
    gb_ref,
    x_ref,
    pack_ref,
    ext,
    sums,
    total,
):
    w2 = w2_ref[...].astype(bf16)
    strip = strip_ref[...].reshape(2 * 48, C)
    for g in range(GROUPS):
        wide = dot(strip, w2[lane_group(g)], NT).reshape(2, 48, LANES)
        wide = (wide * ss_ref[:, :, lane_group(g)].astype(f32)).astype(bf16).astype(f32)
        for row in range(RD + 2):
            ext[g, row, 15:16, :] = wide[0, row : row + 1]
            ext[g, row, 16 + CD : 17 + CD, :] = wide[1, row : row + 1]

    def fill(first, count):
        for k in range(count):
            for g in range(GROUPS):
                part = b_ref[first + k, :, lane_group(g)]
                ext[g, first + k, 16 : 16 + CD, :] = part.astype(f32)

    fill(0, 2)
    sums[...] = jnp.zeros(sums.shape, f32)
    total[...] = jnp.zeros(total.shape, f32)

    def block(i, carry):
        fill(i * 4 + 2, 4)
        for k in range(4):
            row = i * 4 + k
            at = pl.ds(pl.multiple_of(row * CD, CD), CD)
            for g in range(GROUPS):
                own = e_ref[at, lane_group(g)].astype(f32)
                running = None
                for t in range(9):
                    window = ext[g, row + t // 3, 15 + t % 3 : 15 + t % 3 + CD, :]
                    term = dw_ref[8 - t : 9 - t, lane_group(g)] * window
                    running = term if running is None else running + term
                    sums[g, 8 - t] += jnp.sum((own * window).reshape(CD // 8, 8, LANES), axis=0)
                wide = running * s_ref[at, lane_group(g)].astype(f32)
                x_ref[at, lane_group(g)] = wide.astype(bf16)
        four = pl.ds(pl.multiple_of(i * 4 * CD, 4 * CD), 4 * CD)
        normed = n_ref[four, :]
        for g in range(GROUPS):
            total[lane_group(g), :] += dot(normed, x_ref[four, lane_group(g)], TN)
        return carry

    lax.fori_loop(0, RD // 4, block, 0)
    pack_ref[ROW_EXPAND : ROW_EXPAND + E, :] = total[...].astype(bf16)
    pack_ref[ROW_PROJECT : ROW_PROJECT + E, :] = gp_ref[...].astype(bf16)
    pack_ref[ROW_QKV : ROW_QKV + 3 * C, :] = gq_ref[...].astype(bf16)
    pack_ref[ROW_OUT : ROW_OUT + C, :] = go_ref[...].astype(bf16)
    for g in range(GROUPS):
        kernel_sums = jnp.sum(sums[g], axis=1)
        kernel_sums = jnp.concatenate([kernel_sums, jnp.zeros((7, LANES), f32)], axis=0)
        pack_ref[ROW_KERNEL + 16 * g : ROW_KERNEL + 16 * g + 16, :] = kernel_sums.astype(bf16)
    table = jnp.concatenate([gb_ref[:, :LANES], gb_ref[:, LANES:]], axis=0)
    pack_ref[ROW_BIAS : ROW_BIAS + 16, :] = table.astype(bf16)
    pack_ref[ROWS_USED:PACK_ROWS, :] = jnp.zeros((PACK_ROWS - ROWS_USED, C), bf16)


def depth_grad(before, strip, ss, w2, taps, expanded, slope, normed, gp, gq, go, gb):
    tokens = RD * CD
    return pl.pallas_call(
        depth_grad_kernel,
        out_shape=[
            jax.ShapeDtypeStruct((tokens, E), bf16),
            jax.ShapeDtypeStruct((PACK_ROWS, C), bf16),
        ],
        scratch_shapes=[
            pltpu.VMEM((GROUPS, RD + 2, 96, LANES), f32),
            pltpu.VMEM((GROUPS, 9, 8, LANES), f32),
            pltpu.VMEM((E, C), f32),
        ],
        compiler_params=pltpu.CompilerParams(vmem_limit_bytes=VMEM_LIMIT),
        cost_estimate=pl.CostEstimate(
            flops=2 * tokens * C * E + 60 * tokens * E,
            bytes_accessed=tokens * (8 * E + 4 * C),
            transcendentals=0,
        ),
        name="depth_grad",
    )(
        before.reshape(RD + 2, CD, E), strip, ss, w2, taps, expanded, slope, normed, gp, gq, go, gb
    )


def image_grad_kernel(g_ref, w_ref, gain_ref, x_ref, m_ref, o_ref):
    w = w_ref[...].astype(bf16)

    def step(i, carry):
        at = pl.ds(pl.multiple_of(i * 256, 256), 256)
        scaled = dot(g_ref[at, :], w, NT) * gain_ref[...]
        inverse, unit = normalise(x_ref[at, :].astype(f32))
        mean = jnp.mean(scaled * unit, axis=-1, keepdims=True)
        o_ref[at, :] = (m_ref[at, :].astype(f32) + inverse * (scaled - unit * mean)).astype(bf16)
        return carry

    lax.fori_loop(0, x_ref.shape[0] // 256, step, 0)


def image_grad(g, w, gain, x, gm):
    tokens = x.shape[0]
    return pl.pallas_call(
        image_grad_kernel,
        out_shape=jax.ShapeDtypeStruct((tokens, C), bf16),
        compiler_params=pltpu.CompilerParams(vmem_limit_bytes=VMEM_LIMIT),
        cost_estimate=pl.CostEstimate(
            flops=2 * tokens * C * E, bytes_accessed=tokens * (2 * E + 6 * C), transcendentals=0
        ),
        name="image_grad",
    )(g, w, gain, x, gm)


def sum_parts_kernel(factor, x_hbm, o_hbm, x_ref, o_ref, xs, outs):
    x_in = Blocks(x_hbm, x_ref, xs, 32)
    x_in.start_all()
    total = jnp.zeros(x_ref.shape[1:], f32)
    for i in range(4):
        x_in.copy(i).wait()
        for k in range(32):
            total = total + x_ref[32 * i + k].astype(f32)
    total = (total * factor).astype(bf16)
    for k in range(16):
        o_ref[k] = total
    spread = [(o_ref, o_hbm.at[pl.ds(16 * k, 16)]) for k in range(8)]
    spread = copies(spread, outs)
    for copy in spread:
        copy.start()
    for copy in spread:
        copy.wait()


def sum_parts(x, factor):
    return pl.pallas_call(
        lambda *refs: sum_parts_kernel(factor, *refs),
        out_shape=jax.ShapeDtypeStruct(x.shape, bf16),
        in_specs=[HBM],
        out_specs=HBM,
        scratch_shapes=[
            pltpu.VMEM(x.shape, bf16),
            pltpu.VMEM((16,) + x.shape[1:], bf16),
            pltpu.SemaphoreType.DMA((4,)),
            pltpu.SemaphoreType.DMA((8,)),
        ],
        compiler_params=pltpu.CompilerParams(vmem_limit_bytes=VMEM_LIMIT),
        cost_estimate=pl.CostEstimate(
            flops=2 * x.size, bytes_accessed=4 * x.size, transcendentals=0
        ),
        name="sum_parts",
    )(x)


def column_sums(x):
    line = jnp.sum(x, axis=1, keepdims=True)
    return jnp.broadcast_to(line, (C, C)).T[0:1]


def unpack_kernel(
    p_ref, w1_ref, wq_ref, gain1_ref, gain2_ref, g1_ref, ex_ref, k_ref, pr_ref, g2_ref, qk_ref,
    o_ref, b_ref
):
    first = jnp.zeros((C, C), f32)
    second = jnp.zeros((C, C), f32)
    for g in range(GROUPS):
        part = p_ref[ROW_EXPAND + g * C : ROW_EXPAND + (g + 1) * C, :].astype(f32)
        ex_ref[:, lane_group(g)] = part
        first = first + part * w1_ref[:, lane_group(g)].astype(bf16).astype(f32)
        part = p_ref[ROW_PROJECT + g * C : ROW_PROJECT + (g + 1) * C, :].astype(f32)
        pr_ref[g * C : (g + 1) * C, :] = part.T
        part = p_ref[ROW_KERNEL + g * 16 : ROW_KERNEL + (g + 1) * 16, :].astype(f32)
        k_ref[:, lane_group(g)] = part[0:9]
    for k in range(3):
        part = p_ref[ROW_QKV + k * C : ROW_QKV + (k + 1) * C, :].astype(f32)
        qk_ref[:, lane_group(k)] = part
        second = second + part * wq_ref[:, lane_group(k)].astype(bf16).astype(f32)
    g1_ref[...] = column_sums(first) / gain1_ref[...]
    g2_ref[...] = column_sums(second) / gain2_ref[...]
    o_ref[...] = p_ref[ROW_OUT : ROW_OUT + C, :].astype(f32)
    part = p_ref[ROW_BIAS : ROW_BIAS + 16, :].astype(f32)
    table = jnp.concatenate([part[0:4], part[8:12]], axis=1)
    b_ref[...] = jnp.concatenate([table[:, 16 * k : 16 * k + 15] for k in range(15)], axis=1)


def unpack(pack, w1, wq, gain1, gain2):
    return pl.pallas_call(
        unpack_kernel,
        out_shape=[
            jax.ShapeDtypeStruct((1, C), f32),
            jax.ShapeDtypeStruct((C, E), f32),
            jax.ShapeDtypeStruct((9, E), f32),
            jax.ShapeDtypeStruct((E, C), f32),
            jax.ShapeDtypeStruct((1, C), f32),
            jax.ShapeDtypeStruct((C, 3 * C), f32),
            jax.ShapeDtypeStruct((C, C), f32),
            jax.ShapeDtypeStruct((HEADS, 225), f32),
        ],
        compiler_params=pltpu.CompilerParams(vmem_limit_bytes=VMEM_LIMIT),
        cost_estimate=pl.CostEstimate(
            flops=4 * pack.size, bytes_accessed=6 * pack.size, transcendentals=0
        ),
        name="unpack",
    )(pack, w1, wq, gain1, gain2)


def swap_ends(low, high, axis, beside=None):
    count = lax.axis_size(axis)
    odd = lax.axis_index(axis) % 2 == 1
    pairs = [(i, i ^ 1) for i in range(count)]
    others = [(i, ((i - 1) ^ 1) + 1) for i in range(1, count - 1)]
    first = lax.ppermute(jnp.where(odd, low, high), axis, pairs)
    second = lax.ppermute(jnp.where(odd, high, low), axis, others)
    if beside is not None:
        first, beside = lax.optimization_barrier((first, beside))
    ends = jnp.where(odd, first, second), jnp.where(odd, second, first)
    return ends if beside is None else (ends, beside)


def per_device(
    image,
    cotangent,
    norm1_gain,
    w_expand,
    dw_kernel,
    w_project,
    norm2_gain,
    w_qkv,
    w_out,
    bias_table,
):
    factor = 1.0 / math.sqrt(RD * CD * 128)
    w1, w2, wq, wo = w_expand, w_project, w_qkv, w_out
    gain1 = norm1_gain.reshape(1, C)
    gain2 = norm2_gain.reshape(1, C)
    tokens = image.reshape(RD * CD, C)
    above, below = swap_ends(tokens[: 2 * CD], tokens[(RD - 2) * CD :], "rows")
    above = above.reshape(2, CD, C)
    below = below.reshape(2, CD, C)
    left = jnp.concatenate([above[:, :2], image[:, :2], below[:, :2]], axis=0)
    right = jnp.concatenate([above[:, -2:], image[:, -2:], below[:, -2:]], axis=0)
    left = left.transpose(1, 0, 2)
    right = right.transpose(1, 0, 2)
    (before_left, after_right), late_gain = swap_ends(left, right, COLS, gain1)
    expanded, slope1, normed1 = expand(tokens, late_gain, w1)
    halo = jnp.concatenate([above, below], axis=0)
    strip = jnp.concatenate([before_left, left[:1], right[1:], after_right], axis=0)
    strip = jnp.pad(strip, ((0, 0), (0, 12), (0, 0)))
    send, depthed, slope2, slope2_strip = depth(
        expanded, tokens, to_columns(cotangent), halo, strip, gain1, w1, dw_kernel, w2
    )
    windows = lax.all_to_all(send, PLANE, 0, 0, tiled=True)
    back, grad_qkv, grad_out, grad_bias = attend(windows, gain2, wq, wo, bias_table)
    back = lax.all_to_all(back, PLANE, 0, 0, tiled=True)
    grad_left, grad_right = swap_ends(back[0, :40], back[31, 40:80], COLS)
    before, grad_project, grad_middle = project_grad(back, w2, depthed, slope2)
    grad_strip = jnp.pad(jnp.stack([grad_left, grad_right]), ((0, 0), (0, 8), (0, 0)))
    grad_wide, pack = depth_grad(
        before, grad_strip, slope2_strip, w2, dw_kernel, expanded, slope1, normed1,
        grad_project, grad_qkv, grad_out, grad_bias,
    )
    parts = lax.all_to_all(pack.reshape(128, 16, C), ALL, 0, 0, tiled=True)
    grad_wide, parts = lax.optimization_barrier((grad_wide, parts))
    grad_image = image_grad(grad_wide, w1, gain1, tokens, grad_middle)
    block_out = from_columns(back)
    whole = lax.all_to_all(sum_parts(parts, factor), ALL, 0, 0, tiled=True)
    g1, ge, gk, gp, g2, gq, go, gb = unpack(whole.reshape(PACK_ROWS, C), w1, wq, gain1, gain2)
    return (
        block_out,
        grad_image.reshape(RD, CD, C),
        g1.reshape(C),
        ge,
        gk,
        gp,
        g2.reshape(C),
        gq,
        go,
        gb,
    )


def solution(mesh):
    mesh = Mesh(mesh.devices.reshape(4, 8, 4), ALL)
    tiles = P("rows", COLS, None)
    return jax.shard_map(
        per_device,
        mesh=mesh,
        in_specs=(tiles, tiles) + (P(),) * 8,
        out_specs=(tiles, tiles) + (P(),) * 8,
        check_vma=False,
    )
```

```python
import math

import jax
import jax.numpy as jnp
from jax import lax
from jax.experimental import pallas as pl
from jax.experimental.pallas import tpu as pltpu
from jax.sharding import Mesh
from jax.sharding import PartitionSpec as P

GRID = 8
C = 128
E = 512
HEADS = 4
RD = 32
CD = 64
LANES = 128
GROUPS = E // LANES
epsilon = 1e-06
gelu_coef = math.sqrt(2.0 / math.pi)
bf16 = jnp.bfloat16
f32 = jnp.float32
VMEM_LIMIT = 24 * 1024 * 1024

PLANE = ("rows", "group")
COLS = ("group", "plane")
ALL = ("rows", "group", "plane")

ROW_EXPAND = 0
ROW_PROJECT = 512
ROW_QKV = 1024
ROW_OUT = 1408
ROW_KERNEL = 1536
ROW_BIAS = 1600
ROWS_USED = 1616
PACK_ROWS = 2048

PAIRS = 16

HBM = pl.BlockSpec(memory_space=pltpu.HBM)
ANY = pl.BlockSpec()
NT = (((1,), (1,)), ((), ()))
TN = (((0,), (0,)), ((), ()))


def dot(a, b, dims=(((1,), (0,)), ((), ()))):
    return lax.dot_general(a, b, dims, preferred_element_type=f32)


def gelu_value(t):
    t2 = t * t
    u = jnp.tanh(t * (t2 * (0.044715 * gelu_coef) + gelu_coef))
    return t * (0.5 * u + 0.5)


def gelu_pair(t):
    t = t.astype(bf16)
    t2 = t * t
    u = jnp.tanh(t * (t2 * (0.044715 * gelu_coef) + gelu_coef))
    h = 0.5 * u + 0.5
    value = t * h
    slope = h + value * (1.0 - h) * (t2 * (2.0 * 0.134145 * gelu_coef) + 2.0 * gelu_coef)
    return value, slope


def normalise(v):
    inverse = lax.rsqrt(jnp.mean(v * v, axis=-1, keepdims=True) + epsilon)
    return inverse, v * inverse


def rows_of(i, count):
    return pl.ds(pl.multiple_of(i * count, count), count)


def copies(pairs, sems):
    return [pltpu.make_async_copy(a, b, sems.at[k]) for k, (a, b) in enumerate(pairs)]


class Blocks:
    def __init__(self, src, dst, sems, count):
        self.src, self.dst, self.sems, self.count = src, dst, sems, count
        self.steps = src.shape[0] // count

    def copy(self, i):
        at = rows_of(i, self.count) if not isinstance(i, int) else pl.ds(i * self.count, self.count)
        return pltpu.make_async_copy(self.src.at[at], self.dst.at[at], self.sems.at[i])

    def start_all(self):
        for i in range(self.steps):
            self.copy(i).start()

    def wait_all(self):
        for i in range(self.steps):
            self.copy(i).wait()


def lane_group(g):
    return slice(g * LANES, (g + 1) * LANES)


def to_columns_kernel(x_ref, o_ref, rows):
    rows[...] = x_ref[...].reshape(RD * CD, C).astype(f32)
    for col in range(CD):
        part = rows[pl.ds(col, RD, stride=CD), :]
        o_ref[col // 2, (col % 2) * RD : (col % 2 + 1) * RD, :] = part.astype(bf16)


def to_columns(x):
    return pl.pallas_call(
        to_columns_kernel,
        out_shape=jax.ShapeDtypeStruct((CD // 2, 2 * RD, C), bf16),
        scratch_shapes=[pltpu.VMEM((RD * CD, C), f32)],
        compiler_params=pltpu.CompilerParams(vmem_limit_bytes=VMEM_LIMIT),
        cost_estimate=pl.CostEstimate(flops=0, bytes_accessed=4 * RD * CD * C, transcendentals=0),
        name="to_columns",
    )(x)


def from_columns_kernel(x_ref, o_ref, cols):
    cols[...] = x_ref[:, 80:144, :].reshape(RD * CD, C).astype(f32)
    for row in range(RD):
        o_ref[row, :, :] = cols[pl.ds(row, CD, stride=RD), :].astype(bf16)


def from_columns(x):
    return pl.pallas_call(
        from_columns_kernel,
        out_shape=jax.ShapeDtypeStruct((RD, CD, C), bf16),
        scratch_shapes=[pltpu.VMEM((RD * CD, C), f32)],
        compiler_params=pltpu.CompilerParams(vmem_limit_bytes=VMEM_LIMIT),
        cost_estimate=pl.CostEstimate(flops=0, bytes_accessed=4 * RD * CD * C, transcendentals=0),
        name="from_columns",
    )(x)


def expand_kernel(x_ref, gain_ref, w_ref, e_ref, s_ref, n_ref):
    w = w_ref[...].astype(bf16)

    def step(i, carry):
        at = pl.ds(pl.multiple_of(i * 256, 256), 256)
        normed = (normalise(x_ref[at, :].astype(f32))[1] * gain_ref[...]).astype(bf16)
        n_ref[at, :] = normed
        wide = dot(normed, w)
        for g in range(GROUPS):
            value, slope = gelu_pair(wide[:, lane_group(g)])
            e_ref[at, lane_group(g)] = value.astype(bf16)
            s_ref[at, lane_group(g)] = slope.astype(bf16)
        return carry

    lax.fori_loop(0, x_ref.shape[0] // 256, step, 0)


def expand(x, gain, w):
    tokens = x.shape[0]
    return pl.pallas_call(
        expand_kernel,
        out_shape=[
            jax.ShapeDtypeStruct((tokens, E), bf16),
            jax.ShapeDtypeStruct((tokens, E), bf16),
            jax.ShapeDtypeStruct((tokens, C), bf16),
        ],
        compiler_params=pltpu.CompilerParams(vmem_limit_bytes=VMEM_LIMIT),
        cost_estimate=pl.CostEstimate(
            flops=2 * tokens * C * E + 20 * tokens * E,
            bytes_accessed=tokens * (4 * E + 4 * C),
            transcendentals=tokens * E,
        ),
        name="expand",
    )(x, gain, w)


def conv_row(src, taps, g, row):
    total = None
    for a in range(3):
        for b in range(3):
            term = taps[3 * a + b] * src[g, row + a, 15 + b : 15 + b + CD, :]
            total = term if total is None else total + term
    return total


def depth_kernel(
    e_ref,
    x_ref,
    c_ref,
    halo_ref,
    strip_ref,
    gain_ref,
    w1_ref,
    dw_ref,
    w2f_ref,
    send_ref,
    d_ref,
    s_ref,
    ss_ref,
    ext,
    side,
    mid,
    w2_ref,
):
    w2_ref[...] = w2f_ref[...].astype(bf16)
    send_ref[:, 64:128, :] = c_ref[...]
    gain = gain_ref[...]
    halo = normalise(halo_ref[...].reshape(4 * CD, C).astype(f32))[1]
    halo = (halo * gain).astype(bf16)
    strip = normalise(strip_ref[...].reshape(6 * 48, C).astype(f32))[1]
    strip = (strip * gain).astype(bf16)
    for g in range(GROUPS):
        weight = w1_ref[:, lane_group(g)].astype(bf16)
        value = gelu_value(dot(halo, weight)).astype(bf16).astype(f32).reshape(4, CD, C)
        for k, row in enumerate((0, 1, RD + 2, RD + 3)):
            ext[g, row, 16 : 16 + CD, :] = value[k]
        value = gelu_value(dot(strip, weight)).astype(bf16).astype(f32).reshape(6, 48, C)
        side[g, :, 0:48, :] = value
        side[g, :, 48:56, :] = jnp.zeros((6, 8, C), f32)
        for row in range(RD + 4):
            ext[g, row, 15:16, :] = value[1, row : row + 1]
            ext[g, row, 16 + CD : 17 + CD, :] = value[4, row : row + 1]

    def fill(i):
        for k in range(4):
            row = i * 4 + k
            for g in range(GROUPS):
                ext[g, row + 2, 16 : 16 + CD, :] = e_ref[row, :, lane_group(g)].astype(f32)

    def taps_of(g):
        return [dw_ref[t : t + 1, lane_group(g)] for t in range(9)]

    fill(0)

    def project(i):
        four = pl.ds(pl.multiple_of(i * 4 * CD, 4 * CD), 4 * CD)
        mid[four, :] = x_ref[four, :].astype(f32) + dot(d_ref[four, :], w2_ref[...])

    d_ref[0 : 4 * CD, :] = jnp.zeros((4 * CD, E), bf16)

    def block(i, carry):
        @pl.when(i < RD // 4 - 1)
        def _():
            fill(i + 1)

        project(jnp.maximum(i - 1, 0))
        for k in range(4):
            row = i * 4 + k
            at = pl.ds(pl.multiple_of(row * CD, CD), CD)
            ring = pl.ds(pl.multiple_of(row * CD + CD, CD), CD)
            for g in range(GROUPS):
                value, slope = gelu_pair(conv_row(ext, taps_of(g), g, row + 1))
                d_ref[at, lane_group(g)] = value.astype(bf16)
                s_ref[ring, lane_group(g)] = slope.astype(bf16)
        return carry

    lax.fori_loop(0, RD // 4, block, 0)
    project(RD // 4 - 1)
    for col in range(CD):
        part = mid[pl.ds(col, RD, stride=CD), :]
        send_ref[col // 2, (col % 2) * RD : (col % 2 + 1) * RD, :] = part.astype(bf16)
    for g in range(GROUPS):
        taps = taps_of(g)
        for row in (0, RD + 1):
            slope = gelu_pair(conv_row(ext, taps, g, row))[1]
            s_ref[row * CD : (row + 1) * CD, lane_group(g)] = slope.astype(bf16)
        for end in range(2):
            total = None
            for a in range(3):
                for b in range(3):
                    term = taps[3 * a + b] * side[g, 3 * end + b, a : a + 48, :]
                    total = term if total is None else total + term
            ss_ref[end, :, lane_group(g)] = gelu_pair(total)[1].astype(bf16)


def depth(expanded, x, cot, halo, strip, gain, w1, taps, w2):
    tokens = RD * CD
    return pl.pallas_call(
        depth_kernel,
        out_shape=[
            jax.ShapeDtypeStruct((CD // 2, 4 * RD, C), bf16),
            jax.ShapeDtypeStruct((tokens, E), bf16),
            jax.ShapeDtypeStruct((tokens + 2 * CD, E), bf16),
            jax.ShapeDtypeStruct((2, 48, E), bf16),
        ],
        scratch_shapes=[
            pltpu.VMEM((GROUPS, RD + 4, 96, LANES), f32),
            pltpu.VMEM((GROUPS, 6, 56, LANES), f32),
            pltpu.VMEM((tokens, C), f32),
            pltpu.VMEM((E, C), bf16),
        ],
        compiler_params=pltpu.CompilerParams(vmem_limit_bytes=VMEM_LIMIT),
        cost_estimate=pl.CostEstimate(
            flops=2 * tokens * C * E + 40 * tokens * E,
            bytes_accessed=tokens * (6 * E + 4 * C),
            transcendentals=tokens * E,
        ),
        name="depth",
    )(expanded.reshape(RD, CD, E), x, cot, halo, strip, gain, w1, taps, w2)


def side_by_side(x):
    return jnp.concatenate([x[:64], x[64:]], axis=1)


def stacked(x):
    return jnp.concatenate([x[:, :C], x[:, C:]], axis=0)


def diagonal(x):
    return jnp.concatenate([x[:64, :C], x[64:, C:]], axis=0)


def attend_kernel(
    x_ref,
    gain_ref,
    wqf_ref,
    wof_ref,
    table_ref,
    back_ref,
    gq_ref,
    go_ref,
    gb_ref,
    mid,
    cot,
    out,
    grad,
    norms,
    atts,
    cots,
    mixes,
    ds_ref,
    wq_ref,
    wo_ref,
    bias_ref,
):
    spread_table(table_ref, bias_ref)
    grad[...] = jnp.zeros(grad.shape, f32)
    ds_ref[...] = jnp.zeros(ds_ref.shape, f32)
    wq_ref[...] = wqf_ref[...].astype(bf16)
    wo_ref[...] = wof_ref[...].astype(bf16)
    mid[...] = x_ref[:, 0:64, :].reshape(RD * CD, C).astype(f32)
    cot[...] = x_ref[:, 64:128, :].reshape(RD * CD, C).astype(f32)
    gain = gain_ref[...]
    scale = 32**-0.5
    row_head = lax.broadcasted_iota(jnp.int32, (256, 256), 0) // 64
    lane_head = (lax.broadcasted_iota(jnp.int32, (256, 256), 1) % C) // 32
    own_head = row_head == lane_head
    fold_head = (lax.broadcasted_iota(jnp.int32, (64, 256), 1) % C) // 32

    def per_head(x):
        x = side_by_side(x)
        x = jnp.concatenate([x, x, x, x], axis=0)
        return jnp.where(own_head, x, jnp.zeros_like(x))

    def per_window(x):
        none = jnp.zeros((64, C), x.dtype)
        top = jnp.concatenate([x[:64], none], axis=1)
        low = jnp.concatenate([none, x[64:]], axis=1)
        return jnp.concatenate([top, low], axis=0)

    def fold(x):
        total = x[0:64]
        for h in range(1, HEADS):
            total = jnp.where(fold_head == h, x[h * 64 : (h + 1) * 64], total)
        return stacked(total)

    def windows(src, r0, width, first):
        parts = []
        for c in range(2):
            for il in range(2):
                at = pl.ds(c * (width // 2) + il * 16 + first + r0, 32, stride=width)
                parts.append(src[at, :])
        return jnp.concatenate(parts, axis=0)

    def put(dst, r0, width, first, x):
        for c in range(2):
            for il in range(2):
                at = pl.ds(c * (width // 2) + il * 16 + first + r0, 32, stride=width)
                k = 2 * c + il
                dst[at, :] = x[k * 32 : (k + 1) * 32]

    def pairs(i, carry):
        each = range(PAIRS)
        r0s = [i * PAIRS + p for p in each]
        ms = [windows(mid, r0, 64, 0) for r0 in r0s]
        cts = [windows(cot, r0, 64, 0) for r0 in r0s]
        ctbs = [ct.astype(bf16) for ct in cts]
        scales = [normalise(m) for m in ms]
        normed = [(unit * gain).astype(bf16) for _, unit in scales]
        mixture = [dot(n, wq_ref[...]) for n in normed]
        ga = [dot(ct, wo_ref[...], NT).astype(bf16) for ct in ctbs]
        qd = [per_window((x[:, :C] * scale).astype(bf16)) for x in mixture]
        k4 = [per_head(x[:, C : 2 * C].astype(bf16)) for x in mixture]
        v4 = [per_head(x[:, 2 * C :].astype(bf16)) for x in mixture]
        gd = [per_window(x) for x in ga]
        scores = [dot(k4[p], qd[p], NT) for p in each]
        gp = [dot(v4[p], gd[p], NT).reshape(HEADS, 64, 128) for p in each]
        scores = [(x + bias_ref[...]).reshape(HEADS, 64, 128) for x in scores]
        weights = [jnp.exp(x - jnp.max(x, axis=1, keepdims=True)) for x in scores]
        prob = [x * (1.0 / jnp.sum(x, axis=1, keepdims=True)) for x in weights]
        rounded = [x.reshape(256, 128).astype(bf16) for x in prob]
        att = [diagonal(dot(rounded[p], v4[p], TN)).astype(bf16) for p in each]
        gv = [fold(dot(rounded[p], gd[p])) for p in each]
        gs = [
            prob[p] * (gp[p] - jnp.sum(prob[p] * gp[p], axis=1, keepdims=True)) for p in each
        ]
        gs = [x.reshape(256, 128) for x in gs]
        total = gs[0]
        for x in gs[1:]:
            total = total + x
        ds_ref[...] += total
        gr = [x.astype(bf16) for x in gs]
        gk = [fold(dot(gr[p], qd[p])) for p in each]
        gq = [diagonal(dot(gr[p], k4[p], TN)) * scale for p in each]
        gx = [jnp.concatenate([gq[p], gk[p], gv[p]], axis=1).astype(bf16) for p in each]
        gn = [dot(x, wq_ref[...], NT).astype(bf16).astype(f32) for x in gx]
        mixed = [dot(x, wo_ref[...]) for x in att]
        for p in each:
            at = pl.ds(pl.multiple_of(r0s[p] * 128, 128), 128)
            inverse, unit = scales[p]
            scaled = gn[p] * gain
            mean = jnp.mean(scaled * unit, axis=-1, keepdims=True)
            put(grad, r0s[p], 80, 1, cts[p] + inverse * (scaled - unit * mean))
            put(out, r0s[p], 64, 0, ms[p] + mixed[p])
            norms[at, :] = normed[p]
            atts[at, :] = att[p]
            cots[at, :] = ctbs[p]
            mixes[at, :] = gx[p]
        return carry

    lax.fori_loop(0, 16 // PAIRS, pairs, 0)
    for c in range(2):
        low = grad[pl.ds(c * 40 + 32, 24, stride=80), :]
        high = grad[pl.ds(c * 40 + 1 + 8 * 80, 24, stride=80), :]
        grad[pl.ds(c * 40 + 8 * 80, 24, stride=80), :] = low
        grad[pl.ds(c * 40 + 33, 24, stride=80), :] = high
    back_ref[:, 0:80, :] = grad[...].astype(bf16).reshape(32, 80, C)
    back_ref[:, 80:144, :] = out[...].astype(bf16).reshape(32, 64, C)
    gb_ref[...] = table_sums(ds_ref)
    for k in range(3):
        gq_ref[k * C : (k + 1) * C, :] = dot(norms[...], mixes[:, k * C : (k + 1) * C], TN)
    go_ref[...] = dot(atts[...], cots[...], TN)


def place_of(col):
    at = lax.broadcasted_iota(jnp.int32, (128, 128), 0) % 64
    lane = lax.broadcasted_iota(jnp.int32, (128, 128), 1)
    fits = (2 * (at % 32 // 8) + at // 32 == lane // 16) & (at % 8 - col + 7 == lane % 16)
    return jnp.where(fits, 1.0, 0.0).astype(bf16)


def row_of(k):
    return 2 * (k % 4) + k // 4


def spread_table(table_ref, bias_ref):
    none = jnp.zeros((HEADS, 1), f32)
    parts = []
    for k in range(15):
        parts += [table_ref[:, 15 * k : 15 * k + 15], none]
    table = jnp.concatenate(parts + [jnp.zeros((HEADS, 16), f32)], axis=1)
    shifted = [table[:, 16 * (7 - row_of(k)) : 16 * (7 - row_of(k)) + 128] for k in range(8)]
    rows = [shifted[k][h : h + 1] for h in range(HEADS) for k in range(8)]
    rows = jnp.concatenate(rows, axis=0)
    terms = []
    for _ in range(3):
        terms.append(rows.astype(bf16))
        rows = rows - terms[-1].astype(f32)
    terms = jnp.concatenate(terms, axis=0)
    for col in range(8):
        part = dot(terms, place_of(col), NT)
        bias_ref[pl.ds(col, 32, stride=8), :] = part[0:32] + part[32:64] + part[64:96]


def table_sums(ds_ref):
    total = jnp.zeros((32, 128), f32)
    for col in range(8):
        part = ds_ref[pl.ds(col, 32, stride=8), :]
        high = part.astype(bf16)
        rest = (part - high.astype(f32)).astype(bf16)
        both = dot(jnp.concatenate([high, rest], axis=0), place_of(col))
        total = total + both[0:32] + both[32:64]
    rows = []
    for h in range(HEADS):
        row_sum = None
        for k in range(8):
            shift = 16 * (7 - row_of(k))
            part = total[8 * h + k : 8 * h + k + 1]
            none = jnp.zeros((1, 128), f32)
            part = jnp.concatenate([part, none], axis=1)
            part = pltpu.roll(part, shift, 1) if shift else part
            row_sum = part if row_sum is None else row_sum + part
        rows.append(row_sum)
    return jnp.concatenate(rows + [jnp.zeros((4, 256), f32)], axis=0)


def attend(x, gain, wq, wo, table):
    tokens = RD * CD
    return pl.pallas_call(
        attend_kernel,
        out_shape=[
            jax.ShapeDtypeStruct((32, 144, C), bf16),
            jax.ShapeDtypeStruct((3 * C, C), f32),
            jax.ShapeDtypeStruct((C, C), f32),
            jax.ShapeDtypeStruct((8, 256), f32),
        ],
        scratch_shapes=[
            pltpu.VMEM((tokens, C), f32),
            pltpu.VMEM((tokens, C), f32),
            pltpu.VMEM((tokens, C), f32),
            pltpu.VMEM((32 * 80, C), f32),
            pltpu.VMEM((tokens, C), bf16),
            pltpu.VMEM((tokens, C), bf16),
            pltpu.VMEM((tokens, C), bf16),
            pltpu.VMEM((tokens, 3 * C), bf16),
            pltpu.VMEM((256, 128), f32),
            pltpu.VMEM((C, 3 * C), bf16),
            pltpu.VMEM((C, C), bf16),
            pltpu.VMEM((256, 128), f32),
        ],
        compiler_params=pltpu.CompilerParams(vmem_limit_bytes=VMEM_LIMIT),
        cost_estimate=pl.CostEstimate(
            flops=40 * tokens * C * C, bytes_accessed=tokens * 8 * C, transcendentals=tokens * 256
        ),
        name="attend",
    )(x, gain, wq, wo, table)


def project_grad_kernel(g_ref, w2_ref, d_ref, s_ref, b_ref, gp_ref, gm_ref, cols):
    gp_ref[...] = jnp.zeros(gp_ref.shape, f32)
    w2 = w2_ref[...].astype(bf16)
    cols[...] = g_ref[:, 0:80, :].reshape(CD * 40, C).astype(f32)

    def rows(first, count):
        parts = [cols[pl.ds(first + k, CD, stride=40), :] for k in range(count)]
        return jnp.concatenate(parts, axis=0).astype(bf16)

    def before(g, at):
        for k in range(GROUPS):
            wide = dot(g, w2[lane_group(k)], NT)
            wide = wide * s_ref[at, lane_group(k)].astype(f32)
            b_ref[at, lane_group(k)] = wide.astype(bf16)

    def edge(row):
        before(rows(row, 1), pl.ds(row * CD, CD))

    edge(0)
    edge(RD + 1)

    def block(i, carry):
        four = rows_of(i, 4 * CD)
        ring = pl.ds(pl.multiple_of(i * 4 * CD + CD, CD), 4 * CD)
        g = rows(i * 4 + 1, 4)
        gm_ref[four, :] = g
        before(g, ring)
        for k in range(GROUPS):
            gp_ref[lane_group(k), :] += dot(g, d_ref[four, lane_group(k)], TN)
        return carry

    lax.fori_loop(0, RD // 4, block, 0)


def project_grad(gm, w2, depthed, slope):
    tokens = RD * CD
    ring = tokens + 2 * CD
    return pl.pallas_call(
        project_grad_kernel,
        out_shape=[
            jax.ShapeDtypeStruct((ring, E), bf16),
            jax.ShapeDtypeStruct((E, C), f32),
            jax.ShapeDtypeStruct((tokens, C), bf16),
        ],
        scratch_shapes=[pltpu.VMEM((CD * 40, C), f32)],
        compiler_params=pltpu.CompilerParams(vmem_limit_bytes=VMEM_LIMIT),
        cost_estimate=pl.CostEstimate(
            flops=4 * tokens * C * E, bytes_accessed=tokens * (6 * E + 4 * C), transcendentals=0
        ),
        name="project_grad",
    )(gm, w2, depthed, slope)


def depth_grad_kernel(
    b_ref,
    strip_ref,
    ss_ref,
    w2_ref,
    dw_ref,
    e_ref,
    s_ref,
    n_ref,
    gp_ref,
    gq_ref,
    go_ref,
    gb_ref,
    x_ref,
    pack_ref,
    ext,
    sums,
    total,
):
    w2 = w2_ref[...].astype(bf16)
    strip = strip_ref[...].reshape(2 * 48, C)
    for g in range(GROUPS):
        wide = dot(strip, w2[lane_group(g)], NT).reshape(2, 48, LANES)
        wide = (wide * ss_ref[:, :, lane_group(g)].astype(f32)).astype(bf16).astype(f32)
        for row in range(RD + 2):
            ext[g, row, 15:16, :] = wide[0, row : row + 1]
            ext[g, row, 16 + CD : 17 + CD, :] = wide[1, row : row + 1]

    def fill(first, count):
        for k in range(count):
            for g in range(GROUPS):
                part = b_ref[first + k, :, lane_group(g)]
                ext[g, first + k, 16 : 16 + CD, :] = part.astype(f32)

    fill(0, 2)
    sums[...] = jnp.zeros(sums.shape, f32)
    total[...] = jnp.zeros(total.shape, f32)

    def add_grad(i, weight=1.0):
        four = pl.ds(pl.multiple_of(i * 4 * CD, 4 * CD), 4 * CD)
        wide = dot(n_ref[four, :], x_ref[four, :], TN) * weight
        for g in range(GROUPS):
            total[lane_group(g), :] += wide[:, lane_group(g)]

    x_ref[0 : 4 * CD, :] = jnp.zeros((4 * CD, E), bf16)

    def block(i, carry):
        fill(i * 4 + 2, 4)
        add_grad(jnp.maximum(i - 1, 0), jnp.where(i > 0, 1.0, 0.0))
        for k in range(4):
            row = i * 4 + k
            at = pl.ds(pl.multiple_of(row * CD, CD), CD)
            for g in range(GROUPS):
                held = [sums[g, t] for t in range(9)]
                for q in range(0, CD, 16):
                    here = pl.ds(pl.multiple_of(row * CD + q, 16), 16)
                    own = e_ref[here, lane_group(g)].astype(f32)
                    running = None
                    for t in range(9):
                        left = 15 + t % 3 + q
                        window = ext[g, row + t // 3, left : left + 16, :]
                        term = dw_ref[8 - t : 9 - t, lane_group(g)] * window
                        running = term if running is None else running + term
                        part = own * window
                        held[8 - t] = held[8 - t] + (part[0:8] + part[8:16])
                    wide = running * s_ref[here, lane_group(g)].astype(f32)
                    x_ref[here, lane_group(g)] = wide.astype(bf16)
                for t in range(9):
                    sums[g, t] = held[t]
        return carry

    lax.fori_loop(0, RD // 4, block, 0)
    add_grad(RD // 4 - 1)
    pack_ref[ROW_EXPAND : ROW_EXPAND + E, :] = total[...].astype(bf16)
    pack_ref[ROW_PROJECT : ROW_PROJECT + E, :] = gp_ref[...].astype(bf16)
    pack_ref[ROW_QKV : ROW_QKV + 3 * C, :] = gq_ref[...].astype(bf16)
    pack_ref[ROW_OUT : ROW_OUT + C, :] = go_ref[...].astype(bf16)
    for g in range(GROUPS):
        kernel_sums = jnp.sum(sums[g], axis=1)
        kernel_sums = jnp.concatenate([kernel_sums, jnp.zeros((7, LANES), f32)], axis=0)
        pack_ref[ROW_KERNEL + 16 * g : ROW_KERNEL + 16 * g + 16, :] = kernel_sums.astype(bf16)
    table = jnp.concatenate([gb_ref[:, :LANES], gb_ref[:, LANES:]], axis=0)
    pack_ref[ROW_BIAS : ROW_BIAS + 16, :] = table.astype(bf16)
    pack_ref[ROWS_USED:PACK_ROWS, :] = jnp.zeros((PACK_ROWS - ROWS_USED, C), bf16)


def depth_grad(before, strip, ss, w2, taps, expanded, slope, normed, gp, gq, go, gb):
    tokens = RD * CD
    return pl.pallas_call(
        depth_grad_kernel,
        out_shape=[
            jax.ShapeDtypeStruct((tokens, E), bf16),
            jax.ShapeDtypeStruct((PACK_ROWS, C), bf16),
        ],
        scratch_shapes=[
            pltpu.VMEM((GROUPS, RD + 2, 96, LANES), f32),
            pltpu.VMEM((GROUPS, 9, 8, LANES), f32),
            pltpu.VMEM((E, C), f32),
        ],
        compiler_params=pltpu.CompilerParams(vmem_limit_bytes=VMEM_LIMIT),
        cost_estimate=pl.CostEstimate(
            flops=2 * tokens * C * E + 60 * tokens * E,
            bytes_accessed=tokens * (8 * E + 4 * C),
            transcendentals=0,
        ),
        name="depth_grad",
    )(
        before.reshape(RD + 2, CD, E), strip, ss, w2, taps, expanded, slope, normed, gp, gq, go, gb
    )


def image_grad_kernel(g_ref, w_ref, gain_ref, x_ref, m_ref, o_ref):
    w = w_ref[...].astype(bf16)

    def step(i, carry):
        at = pl.ds(pl.multiple_of(i * 256, 256), 256)
        scaled = dot(g_ref[at, :], w, NT) * gain_ref[...]
        inverse, unit = normalise(x_ref[at, :].astype(f32))
        mean = jnp.mean(scaled * unit, axis=-1, keepdims=True)
        o_ref[at, :] = (m_ref[at, :].astype(f32) + inverse * (scaled - unit * mean)).astype(bf16)
        return carry

    lax.fori_loop(0, x_ref.shape[0] // 256, step, 0)


def image_grad(g, w, gain, x, gm):
    tokens = x.shape[0]
    return pl.pallas_call(
        image_grad_kernel,
        out_shape=jax.ShapeDtypeStruct((tokens, C), bf16),
        compiler_params=pltpu.CompilerParams(vmem_limit_bytes=VMEM_LIMIT),
        cost_estimate=pl.CostEstimate(
            flops=2 * tokens * C * E, bytes_accessed=tokens * (2 * E + 6 * C), transcendentals=0
        ),
        name="image_grad",
    )(g, w, gain, x, gm)


def sum_parts_kernel(factor, x_hbm, o_hbm, x_ref, o_ref, xs, outs):
    x_in = Blocks(x_hbm, x_ref, xs, 32)
    x_in.start_all()
    total = jnp.zeros(x_ref.shape[1:], f32)
    for i in range(4):
        x_in.copy(i).wait()
        for k in range(32):
            total = total + x_ref[32 * i + k].astype(f32)
    total = (total * factor).astype(bf16)
    for k in range(16):
        o_ref[k] = total
    spread = [(o_ref, o_hbm.at[pl.ds(16 * k, 16)]) for k in range(8)]
    spread = copies(spread, outs)
    for copy in spread:
        copy.start()
    for copy in spread:
        copy.wait()


def sum_parts(x, factor):
    return pl.pallas_call(
        lambda *refs: sum_parts_kernel(factor, *refs),
        out_shape=jax.ShapeDtypeStruct(x.shape, bf16),
        in_specs=[HBM],
        out_specs=HBM,
        scratch_shapes=[
            pltpu.VMEM(x.shape, bf16),
            pltpu.VMEM((16,) + x.shape[1:], bf16),
            pltpu.SemaphoreType.DMA((4,)),
            pltpu.SemaphoreType.DMA((8,)),
        ],
        compiler_params=pltpu.CompilerParams(vmem_limit_bytes=VMEM_LIMIT),
        cost_estimate=pl.CostEstimate(
            flops=2 * x.size, bytes_accessed=4 * x.size, transcendentals=0
        ),
        name="sum_parts",
    )(x)


def column_sums(x):
    line = jnp.sum(x, axis=1, keepdims=True)
    return jnp.broadcast_to(line, (C, C)).T[0:1]


def unpack_kernel(
    p_ref, w1_ref, wq_ref, gain1_ref, gain2_ref, g1_ref, ex_ref, k_ref, pr_ref, g2_ref, qk_ref,
    o_ref, b_ref
):
    first = jnp.zeros((C, C), f32)
    second = jnp.zeros((C, C), f32)
    for g in range(GROUPS):
        part = p_ref[ROW_EXPAND + g * C : ROW_EXPAND + (g + 1) * C, :].astype(f32)
        ex_ref[:, lane_group(g)] = part
        first = first + part * w1_ref[:, lane_group(g)].astype(bf16).astype(f32)
        part = p_ref[ROW_PROJECT + g * C : ROW_PROJECT + (g + 1) * C, :].astype(f32)
        pr_ref[g * C : (g + 1) * C, :] = part.T
        part = p_ref[ROW_KERNEL + g * 16 : ROW_KERNEL + (g + 1) * 16, :].astype(f32)
        k_ref[:, lane_group(g)] = part[0:9]
    for k in range(3):
        part = p_ref[ROW_QKV + k * C : ROW_QKV + (k + 1) * C, :].astype(f32)
        qk_ref[:, lane_group(k)] = part
        second = second + part * wq_ref[:, lane_group(k)].astype(bf16).astype(f32)
    g1_ref[...] = column_sums(first) / gain1_ref[...]
    g2_ref[...] = column_sums(second) / gain2_ref[...]
    o_ref[...] = p_ref[ROW_OUT : ROW_OUT + C, :].astype(f32)
    part = p_ref[ROW_BIAS : ROW_BIAS + 16, :].astype(f32)
    table = jnp.concatenate([part[0:4], part[8:12]], axis=1)
    b_ref[...] = jnp.concatenate([table[:, 16 * k : 16 * k + 15] for k in range(15)], axis=1)


def unpack(pack, w1, wq, gain1, gain2):
    return pl.pallas_call(
        unpack_kernel,
        out_shape=[
            jax.ShapeDtypeStruct((1, C), f32),
            jax.ShapeDtypeStruct((C, E), f32),
            jax.ShapeDtypeStruct((9, E), f32),
            jax.ShapeDtypeStruct((E, C), f32),
            jax.ShapeDtypeStruct((1, C), f32),
            jax.ShapeDtypeStruct((C, 3 * C), f32),
            jax.ShapeDtypeStruct((C, C), f32),
            jax.ShapeDtypeStruct((HEADS, 225), f32),
        ],
        compiler_params=pltpu.CompilerParams(vmem_limit_bytes=VMEM_LIMIT),
        cost_estimate=pl.CostEstimate(
            flops=4 * pack.size, bytes_accessed=6 * pack.size, transcendentals=0
        ),
        name="unpack",
    )(pack, w1, wq, gain1, gain2)


def swap_ends(low, high, axis, beside=None):
    count = lax.axis_size(axis)
    odd = lax.axis_index(axis) % 2 == 1
    pairs = [(i, i ^ 1) for i in range(count)]
    others = [(i, ((i - 1) ^ 1) + 1) for i in range(1, count - 1)]
    first = lax.ppermute(jnp.where(odd, low, high), axis, pairs)
    second = lax.ppermute(jnp.where(odd, high, low), axis, others)
    if beside is not None:
        first, beside = lax.optimization_barrier((first, beside))
    ends = jnp.where(odd, first, second), jnp.where(odd, second, first)
    return ends if beside is None else (ends, beside)


def per_device(
    image,
    cotangent,
    norm1_gain,
    w_expand,
    dw_kernel,
    w_project,
    norm2_gain,
    w_qkv,
    w_out,
    bias_table,
):
    factor = 1.0 / math.sqrt(RD * CD * 128)
    w1, w2, wq, wo = w_expand, w_project, w_qkv, w_out
    gain1 = norm1_gain.reshape(1, C)
    gain2 = norm2_gain.reshape(1, C)
    tokens = image.reshape(RD * CD, C)
    above, below = swap_ends(tokens[: 2 * CD], tokens[(RD - 2) * CD :], "rows")
    above = above.reshape(2, CD, C)
    below = below.reshape(2, CD, C)
    left = jnp.concatenate([above[:, :2], image[:, :2], below[:, :2]], axis=0)
    right = jnp.concatenate([above[:, -2:], image[:, -2:], below[:, -2:]], axis=0)
    left = left.transpose(1, 0, 2)
    right = right.transpose(1, 0, 2)
    (before_left, after_right), late_gain = swap_ends(left, right, COLS, gain1)
    expanded, slope1, normed1 = expand(tokens, late_gain, w1)
    halo = jnp.concatenate([above, below], axis=0)
    strip = jnp.concatenate([before_left, left[:1], right[1:], after_right], axis=0)
    strip = jnp.pad(strip, ((0, 0), (0, 12), (0, 0)))
    send, depthed, slope2, slope2_strip = depth(
        expanded, tokens, to_columns(cotangent), halo, strip, gain1, w1, dw_kernel, w2
    )
    windows = lax.all_to_all(send, PLANE, 0, 0, tiled=True)
    back, grad_qkv, grad_out, grad_bias = attend(windows, gain2, wq, wo, bias_table)
    back = lax.all_to_all(back, PLANE, 0, 0, tiled=True)
    grad_left, grad_right = swap_ends(back[0, :40], back[31, 40:80], COLS)
    before, grad_project, grad_middle = project_grad(back, w2, depthed, slope2)
    grad_strip = jnp.pad(jnp.stack([grad_left, grad_right]), ((0, 0), (0, 8), (0, 0)))
    grad_wide, pack = depth_grad(
        before, grad_strip, slope2_strip, w2, dw_kernel, expanded, slope1, normed1,
        grad_project, grad_qkv, grad_out, grad_bias,
    )
    parts = lax.all_to_all(pack.reshape(128, 16, C), ALL, 0, 0, tiled=True)
    grad_wide, parts = lax.optimization_barrier((grad_wide, parts))
    grad_image = image_grad(grad_wide, w1, gain1, tokens, grad_middle)
    block_out = from_columns(back)
    whole = lax.all_to_all(sum_parts(parts, factor), ALL, 0, 0, tiled=True)
    g1, ge, gk, gp, g2, gq, go, gb = unpack(whole.reshape(PACK_ROWS, C), w1, wq, gain1, gain2)
    return (
        block_out,
        grad_image.reshape(RD, CD, C),
        g1.reshape(C),
        ge,
        gk,
        gp,
        g2.reshape(C),
        gq,
        go,
        gb,
    )


def solution(mesh):
    mesh = Mesh(mesh.devices.reshape(4, 8, 4), ALL)
    tiles = P("rows", COLS, None)
    return jax.shard_map(
        per_device,
        mesh=mesh,
        in_specs=(tiles, tiles) + (P(),) * 8,
        out_specs=(tiles, tiles) + (P(),) * 8,
        check_vma=False,
    )
```

```python
import math

import jax
import jax.numpy as jnp
from jax import lax
from jax.experimental import pallas as pl
from jax.experimental.pallas import tpu as pltpu
from jax.sharding import Mesh
from jax.sharding import PartitionSpec as P

GRID = 8
C = 128
E = 512
HEADS = 4
RD = 32
CD = 64
LANES = 128
GROUPS = E // LANES
epsilon = 1e-06
gelu_coef = math.sqrt(2.0 / math.pi)
bf16 = jnp.bfloat16
f32 = jnp.float32
VMEM_LIMIT = 24 * 1024 * 1024

PLANE = ("rows", "group")
COLS = ("group", "plane")
ALL = ("rows", "group", "plane")

ROW_EXPAND = 0
ROW_PROJECT = 512
ROW_QKV = 1024
ROW_OUT = 1408
ROW_KERNEL = 1536
ROW_BIAS = 1600
ROWS_USED = 1616
PACK_ROWS = 2048

HBM = pl.BlockSpec(memory_space=pltpu.HBM)
ANY = pl.BlockSpec()
NT = (((1,), (1,)), ((), ()))
TN = (((0,), (0,)), ((), ()))


def dot(a, b, dims=(((1,), (0,)), ((), ()))):
    return lax.dot_general(a, b, dims, preferred_element_type=f32)


def gelu_value(t):
    t2 = t * t
    u = jnp.tanh(t * (t2 * (0.044715 * gelu_coef) + gelu_coef))
    return t * (0.5 * u + 0.5)


def gelu_pair(t):
    t = t.astype(bf16)
    t2 = t * t
    u = jnp.tanh(t * (t2 * (0.044715 * gelu_coef) + gelu_coef))
    h = 0.5 * u + 0.5
    value = t * h
    slope = h + value * (1.0 - h) * (t2 * (2.0 * 0.134145 * gelu_coef) + 2.0 * gelu_coef)
    return value, slope


def normalise(v):
    inverse = lax.rsqrt(jnp.mean(v * v, axis=-1, keepdims=True) + epsilon)
    return inverse, v * inverse


def rows_of(i, count):
    return pl.ds(pl.multiple_of(i * count, count), count)


def copies(pairs, sems):
    return [pltpu.make_async_copy(a, b, sems.at[k]) for k, (a, b) in enumerate(pairs)]


class Blocks:
    def __init__(self, src, dst, sems, count):
        self.src, self.dst, self.sems, self.count = src, dst, sems, count
        self.steps = src.shape[0] // count

    def copy(self, i):
        at = rows_of(i, self.count) if not isinstance(i, int) else pl.ds(i * self.count, self.count)
        return pltpu.make_async_copy(self.src.at[at], self.dst.at[at], self.sems.at[i])

    def start_all(self):
        for i in range(self.steps):
            self.copy(i).start()

    def wait_all(self):
        for i in range(self.steps):
            self.copy(i).wait()


def lane_group(g):
    return slice(g * LANES, (g + 1) * LANES)


def to_columns_kernel(x_ref, o_ref, rows):
    rows[...] = x_ref[...].reshape(RD * CD, C).astype(f32)
    for col in range(CD):
        part = rows[pl.ds(col, RD, stride=CD), :]
        o_ref[col // 2, (col % 2) * RD : (col % 2 + 1) * RD, :] = part.astype(bf16)


def to_columns(x):
    return pl.pallas_call(
        to_columns_kernel,
        out_shape=jax.ShapeDtypeStruct((CD // 2, 2 * RD, C), bf16),
        scratch_shapes=[pltpu.VMEM((RD * CD, C), f32)],
        compiler_params=pltpu.CompilerParams(vmem_limit_bytes=VMEM_LIMIT),
        cost_estimate=pl.CostEstimate(flops=0, bytes_accessed=4 * RD * CD * C, transcendentals=0),
        name="to_columns",
    )(x)


def from_columns_kernel(x_ref, o_ref, cols):
    cols[...] = x_ref[:, 80:144, :].reshape(RD * CD, C).astype(f32)
    for row in range(RD):
        o_ref[row, :, :] = cols[pl.ds(row, CD, stride=RD), :].astype(bf16)


def from_columns(x):
    return pl.pallas_call(
        from_columns_kernel,
        out_shape=jax.ShapeDtypeStruct((RD, CD, C), bf16),
        scratch_shapes=[pltpu.VMEM((RD * CD, C), f32)],
        compiler_params=pltpu.CompilerParams(vmem_limit_bytes=VMEM_LIMIT),
        cost_estimate=pl.CostEstimate(flops=0, bytes_accessed=4 * RD * CD * C, transcendentals=0),
        name="from_columns",
    )(x)


def expand_kernel(x_ref, gain_ref, w_ref, e_ref, s_ref, n_ref):
    w = w_ref[...].astype(bf16)

    def step(i, carry):
        at = pl.ds(pl.multiple_of(i * 256, 256), 256)
        normed = (normalise(x_ref[at, :].astype(f32))[1] * gain_ref[...]).astype(bf16)
        n_ref[at, :] = normed
        wide = dot(normed, w)
        for g in range(GROUPS):
            value, slope = gelu_pair(wide[:, lane_group(g)])
            e_ref[at, lane_group(g)] = value.astype(bf16)
            s_ref[at, lane_group(g)] = slope.astype(bf16)
        return carry

    lax.fori_loop(0, x_ref.shape[0] // 256, step, 0)


def expand(x, gain, w):
    tokens = x.shape[0]
    return pl.pallas_call(
        expand_kernel,
        out_shape=[
            jax.ShapeDtypeStruct((tokens, E), bf16),
            jax.ShapeDtypeStruct((tokens, E), bf16),
            jax.ShapeDtypeStruct((tokens, C), bf16),
        ],
        compiler_params=pltpu.CompilerParams(vmem_limit_bytes=VMEM_LIMIT),
        cost_estimate=pl.CostEstimate(
            flops=2 * tokens * C * E + 20 * tokens * E,
            bytes_accessed=tokens * (4 * E + 4 * C),
            transcendentals=tokens * E,
        ),
        name="expand",
    )(x, gain, w)


def conv_row(src, taps, g, row):
    total = None
    for a in range(3):
        for b in range(3):
            term = taps[3 * a + b] * src[g, row + a, 15 + b : 15 + b + CD, :]
            total = term if total is None else total + term
    return total


def depth_kernel(
    e_ref,
    x_ref,
    c_ref,
    halo_ref,
    strip_ref,
    gain_ref,
    w1_ref,
    dw_ref,
    w2f_ref,
    send_ref,
    d_ref,
    s_ref,
    ss_ref,
    ext,
    side,
    mid,
    w2_ref,
):
    w2_ref[...] = w2f_ref[...].astype(bf16)
    send_ref[:, 64:128, :] = c_ref[...]
    gain = gain_ref[...]
    halo = normalise(halo_ref[...].reshape(4 * CD, C).astype(f32))[1]
    halo = (halo * gain).astype(bf16)
    strip = normalise(strip_ref[...].reshape(6 * 48, C).astype(f32))[1]
    strip = (strip * gain).astype(bf16)
    for g in range(GROUPS):
        weight = w1_ref[:, lane_group(g)].astype(bf16)
        value = gelu_value(dot(halo, weight)).astype(bf16).astype(f32).reshape(4, CD, C)
        for k, row in enumerate((0, 1, RD + 2, RD + 3)):
            ext[g, row, 16 : 16 + CD, :] = value[k]
        value = gelu_value(dot(strip, weight)).astype(bf16).astype(f32).reshape(6, 48, C)
        side[g, :, 0:48, :] = value
        side[g, :, 48:56, :] = jnp.zeros((6, 8, C), f32)
        for row in range(RD + 4):
            ext[g, row, 15:16, :] = value[1, row : row + 1]
            ext[g, row, 16 + CD : 17 + CD, :] = value[4, row : row + 1]

    def fill(i):
        for k in range(4):
            row = i * 4 + k
            for g in range(GROUPS):
                ext[g, row + 2, 16 : 16 + CD, :] = e_ref[row, :, lane_group(g)].astype(f32)

    def taps_of(g):
        return [dw_ref[t : t + 1, lane_group(g)] for t in range(9)]

    fill(0)

    def project(i):
        four = pl.ds(pl.multiple_of(i * 4 * CD, 4 * CD), 4 * CD)
        mid[four, :] = x_ref[four, :].astype(f32) + dot(d_ref[four, :], w2_ref[...])

    d_ref[0 : 4 * CD, :] = jnp.zeros((4 * CD, E), bf16)

    def block(i, carry):
        @pl.when(i < RD // 4 - 1)
        def _():
            fill(i + 1)

        project(jnp.maximum(i - 1, 0))
        for k in range(4):
            row = i * 4 + k
            at = pl.ds(pl.multiple_of(row * CD, CD), CD)
            ring = pl.ds(pl.multiple_of(row * CD + CD, CD), CD)
            for g in range(GROUPS):
                value, slope = gelu_pair(conv_row(ext, taps_of(g), g, row + 1))
                d_ref[at, lane_group(g)] = value.astype(bf16)
                s_ref[ring, lane_group(g)] = slope.astype(bf16)
        return carry

    lax.fori_loop(0, RD // 4, block, 0)
    project(RD // 4 - 1)
    for col in range(CD):
        part = mid[pl.ds(col, RD, stride=CD), :]
        send_ref[col // 2, (col % 2) * RD : (col % 2 + 1) * RD, :] = part.astype(bf16)
    for g in range(GROUPS):
        taps = taps_of(g)
        for row in (0, RD + 1):
            slope = gelu_pair(conv_row(ext, taps, g, row))[1]
            s_ref[row * CD : (row + 1) * CD, lane_group(g)] = slope.astype(bf16)
        for end in range(2):
            total = None
            for a in range(3):
                for b in range(3):
                    term = taps[3 * a + b] * side[g, 3 * end + b, a : a + 48, :]
                    total = term if total is None else total + term
            ss_ref[end, :, lane_group(g)] = gelu_pair(total)[1].astype(bf16)


def depth(expanded, x, cot, halo, strip, gain, w1, taps, w2):
    tokens = RD * CD
    return pl.pallas_call(
        depth_kernel,
        out_shape=[
            jax.ShapeDtypeStruct((CD // 2, 4 * RD, C), bf16),
            jax.ShapeDtypeStruct((tokens, E), bf16),
            jax.ShapeDtypeStruct((tokens + 2 * CD, E), bf16),
            jax.ShapeDtypeStruct((2, 48, E), bf16),
        ],
        scratch_shapes=[
            pltpu.VMEM((GROUPS, RD + 4, 96, LANES), f32),
            pltpu.VMEM((GROUPS, 6, 56, LANES), f32),
            pltpu.VMEM((tokens, C), f32),
            pltpu.VMEM((E, C), bf16),
        ],
        compiler_params=pltpu.CompilerParams(vmem_limit_bytes=VMEM_LIMIT),
        cost_estimate=pl.CostEstimate(
            flops=2 * tokens * C * E + 40 * tokens * E,
            bytes_accessed=tokens * (6 * E + 4 * C),
            transcendentals=tokens * E,
        ),
        name="depth",
    )(expanded.reshape(RD, CD, E), x, cot, halo, strip, gain, w1, taps, w2)


def side_by_side(x):
    return jnp.concatenate([x[:64], x[64:]], axis=1)


def stacked(x):
    return jnp.concatenate([x[:, :C], x[:, C:]], axis=0)


def diagonal(x):
    return jnp.concatenate([x[:64, :C], x[64:, C:]], axis=0)


def attend_kernel(
    x_ref,
    gain_ref,
    wqf_ref,
    wof_ref,
    table_ref,
    back_ref,
    gq_ref,
    go_ref,
    gb_ref,
    mid,
    cot,
    out,
    grad,
    norms,
    atts,
    cots,
    mixes,
    ds_ref,
    wq_ref,
    wo_ref,
    bias_ref,
):
    spread_table(table_ref, bias_ref)
    grad[...] = jnp.zeros(grad.shape, f32)
    ds_ref[...] = jnp.zeros(ds_ref.shape, f32)
    wq_ref[...] = wqf_ref[...].astype(bf16)
    wo_ref[...] = wof_ref[...].astype(bf16)
    mid[...] = x_ref[:, 0:64, :].reshape(RD * CD, C).astype(f32)
    cot[...] = x_ref[:, 64:128, :].reshape(RD * CD, C).astype(f32)
    gain = gain_ref[...]
    scale = 32**-0.5
    row_head = lax.broadcasted_iota(jnp.int32, (256, 256), 0) // 64
    lane_head = (lax.broadcasted_iota(jnp.int32, (256, 256), 1) % C) // 32
    own_head = row_head == lane_head
    fold_head = (lax.broadcasted_iota(jnp.int32, (64, 256), 1) % C) // 32

    def per_head(x):
        x = side_by_side(x)
        x = jnp.concatenate([x, x, x, x], axis=0)
        return jnp.where(own_head, x, jnp.zeros_like(x))

    def per_window(x):
        none = jnp.zeros((64, C), x.dtype)
        top = jnp.concatenate([x[:64], none], axis=1)
        low = jnp.concatenate([none, x[64:]], axis=1)
        return jnp.concatenate([top, low], axis=0)

    def fold(x):
        total = x[0:64]
        for h in range(1, HEADS):
            total = jnp.where(fold_head == h, x[h * 64 : (h + 1) * 64], total)
        return stacked(total)

    def windows(src, r0, width, first):
        parts = []
        for c in range(2):
            for il in range(2):
                at = pl.ds(c * (width // 2) + il * 16 + first + r0, 32, stride=width)
                parts.append(src[at, :])
        return jnp.concatenate(parts, axis=0)

    def put(dst, r0, width, first, x):
        for c in range(2):
            for il in range(2):
                at = pl.ds(c * (width // 2) + il * 16 + first + r0, 32, stride=width)
                k = 2 * c + il
                dst[at, :] = x[k * 32 : (k + 1) * 32]

    def pairs(r0s):
        each = range(len(r0s))
        ms = [windows(mid, r0, 64, 0) for r0 in r0s]
        cts = [windows(cot, r0, 64, 0) for r0 in r0s]
        ctbs = [ct.astype(bf16) for ct in cts]
        scales = [normalise(m) for m in ms]
        normed = [(unit * gain).astype(bf16) for _, unit in scales]
        mixture = [dot(n, wq_ref[...]) for n in normed]
        ga = [dot(ct, wo_ref[...], NT).astype(bf16) for ct in ctbs]
        qd = [per_window((x[:, :C] * scale).astype(bf16)) for x in mixture]
        k4 = [per_head(x[:, C : 2 * C].astype(bf16)) for x in mixture]
        v4 = [per_head(x[:, 2 * C :].astype(bf16)) for x in mixture]
        gd = [per_window(x) for x in ga]
        scores = [dot(k4[p], qd[p], NT) for p in each]
        gp = [dot(v4[p], gd[p], NT).reshape(HEADS, 64, 128) for p in each]
        scores = [(x + bias_ref[...]).reshape(HEADS, 64, 128) for x in scores]
        weights = [jnp.exp(x - jnp.max(x, axis=1, keepdims=True)) for x in scores]
        prob = [x * (1.0 / jnp.sum(x, axis=1, keepdims=True)) for x in weights]
        rounded = [x.reshape(256, 128).astype(bf16) for x in prob]
        att = [diagonal(dot(rounded[p], v4[p], TN)).astype(bf16) for p in each]
        gv = [fold(dot(rounded[p], gd[p])) for p in each]
        gs = [
            prob[p] * (gp[p] - jnp.sum(prob[p] * gp[p], axis=1, keepdims=True)) for p in each
        ]
        gs = [x.reshape(256, 128) for x in gs]
        total = gs[0]
        for x in gs[1:]:
            total = total + x
        ds_ref[...] += total
        gr = [x.astype(bf16) for x in gs]
        gk = [fold(dot(gr[p], qd[p])) for p in each]
        gq = [diagonal(dot(gr[p], k4[p], TN)) * scale for p in each]
        gx = [jnp.concatenate([gq[p], gk[p], gv[p]], axis=1).astype(bf16) for p in each]
        gn = [dot(x, wq_ref[...], NT).astype(bf16).astype(f32) for x in gx]
        mixed = [dot(x, wo_ref[...]) for x in att]
        for p in each:
            at = pl.ds(r0s[p] * 128, 128)
            inverse, unit = scales[p]
            scaled = gn[p] * gain
            mean = jnp.mean(scaled * unit, axis=-1, keepdims=True)
            put(grad, r0s[p], 80, 1, cts[p] + inverse * (scaled - unit * mean))
            put(out, r0s[p], 64, 0, ms[p] + mixed[p])
            norms[at, :] = normed[p]
            atts[at, :] = att[p]
            cots[at, :] = ctbs[p]
            mixes[at, :] = gx[p]

    pairs(range(16))
    for c in range(2):
        low = grad[pl.ds(c * 40 + 32, 24, stride=80), :]
        high = grad[pl.ds(c * 40 + 1 + 8 * 80, 24, stride=80), :]
        grad[pl.ds(c * 40 + 8 * 80, 24, stride=80), :] = low
        grad[pl.ds(c * 40 + 33, 24, stride=80), :] = high
    back_ref[:, 0:80, :] = grad[...].astype(bf16).reshape(32, 80, C)
    back_ref[:, 80:144, :] = out[...].astype(bf16).reshape(32, 64, C)
    gb_ref[...] = table_sums(ds_ref)
    for k in range(3):
        gq_ref[k * C : (k + 1) * C, :] = dot(norms[...], mixes[:, k * C : (k + 1) * C], TN)
    go_ref[...] = dot(atts[...], cots[...], TN)


def place_of(col):
    at = lax.broadcasted_iota(jnp.int32, (128, 128), 0) % 64
    lane = lax.broadcasted_iota(jnp.int32, (128, 128), 1)
    fits = (2 * (at % 32 // 8) + at // 32 == lane // 16) & (at % 8 - col + 7 == lane % 16)
    return jnp.where(fits, 1.0, 0.0).astype(bf16)


def row_of(k):
    return 2 * (k % 4) + k // 4


def spread_table(table_ref, bias_ref):
    none = jnp.zeros((HEADS, 1), f32)
    parts = []
    for k in range(15):
        parts += [table_ref[:, 15 * k : 15 * k + 15], none]
    table = jnp.concatenate(parts + [jnp.zeros((HEADS, 16), f32)], axis=1)
    shifted = [table[:, 16 * (7 - row_of(k)) : 16 * (7 - row_of(k)) + 128] for k in range(8)]
    rows = [shifted[k][h : h + 1] for h in range(HEADS) for k in range(8)]
    rows = jnp.concatenate(rows, axis=0)
    terms = []
    for _ in range(3):
        terms.append(rows.astype(bf16))
        rows = rows - terms[-1].astype(f32)
    terms = jnp.concatenate(terms, axis=0)
    for col in range(8):
        part = dot(terms, place_of(col), NT)
        bias_ref[pl.ds(col, 32, stride=8), :] = part[0:32] + part[32:64] + part[64:96]


def table_sums(ds_ref):
    total = jnp.zeros((32, 128), f32)
    for col in range(8):
        part = ds_ref[pl.ds(col, 32, stride=8), :]
        high = part.astype(bf16)
        rest = (part - high.astype(f32)).astype(bf16)
        both = dot(jnp.concatenate([high, rest], axis=0), place_of(col))
        total = total + both[0:32] + both[32:64]
    rows = []
    for h in range(HEADS):
        row_sum = None
        for k in range(8):
            shift = 16 * (7 - row_of(k))
            part = total[8 * h + k : 8 * h + k + 1]
            none = jnp.zeros((1, 128), f32)
            part = jnp.concatenate([part, none], axis=1)
            part = pltpu.roll(part, shift, 1) if shift else part
            row_sum = part if row_sum is None else row_sum + part
        rows.append(row_sum)
    return jnp.concatenate(rows + [jnp.zeros((4, 256), f32)], axis=0)


def attend(x, gain, wq, wo, table):
    tokens = RD * CD
    return pl.pallas_call(
        attend_kernel,
        out_shape=[
            jax.ShapeDtypeStruct((32, 144, C), bf16),
            jax.ShapeDtypeStruct((3 * C, C), f32),
            jax.ShapeDtypeStruct((C, C), f32),
            jax.ShapeDtypeStruct((8, 256), f32),
        ],
        scratch_shapes=[
            pltpu.VMEM((tokens, C), f32),
            pltpu.VMEM((tokens, C), f32),
            pltpu.VMEM((tokens, C), f32),
            pltpu.VMEM((32 * 80, C), f32),
            pltpu.VMEM((tokens, C), bf16),
            pltpu.VMEM((tokens, C), bf16),
            pltpu.VMEM((tokens, C), bf16),
            pltpu.VMEM((tokens, 3 * C), bf16),
            pltpu.VMEM((256, 128), f32),
            pltpu.VMEM((C, 3 * C), bf16),
            pltpu.VMEM((C, C), bf16),
            pltpu.VMEM((256, 128), f32),
        ],
        compiler_params=pltpu.CompilerParams(vmem_limit_bytes=VMEM_LIMIT),
        cost_estimate=pl.CostEstimate(
            flops=40 * tokens * C * C, bytes_accessed=tokens * 8 * C, transcendentals=tokens * 256
        ),
        name="attend",
    )(x, gain, wq, wo, table)


def project_grad_kernel(g_ref, w2_ref, d_ref, s_ref, b_ref, gp_ref, gm_ref, cols):
    gp_ref[...] = jnp.zeros(gp_ref.shape, f32)
    w2 = w2_ref[...].astype(bf16)
    cols[...] = g_ref[:, 0:80, :].reshape(CD * 40, C).astype(f32)

    def rows(first, count):
        parts = [cols[pl.ds(first + k, CD, stride=40), :] for k in range(count)]
        return jnp.concatenate(parts, axis=0).astype(bf16)

    def before(g, at):
        for k in range(GROUPS):
            wide = dot(g, w2[lane_group(k)], NT)
            wide = wide * s_ref[at, lane_group(k)].astype(f32)
            b_ref[at, lane_group(k)] = wide.astype(bf16)

    def edge(row):
        before(rows(row, 1), pl.ds(row * CD, CD))

    edge(0)
    edge(RD + 1)

    def block(i, carry):
        four = rows_of(i, 4 * CD)
        ring = pl.ds(pl.multiple_of(i * 4 * CD + CD, CD), 4 * CD)
        g = rows(i * 4 + 1, 4)
        gm_ref[four, :] = g
        before(g, ring)
        for k in range(GROUPS):
            gp_ref[lane_group(k), :] += dot(g, d_ref[four, lane_group(k)], TN)
        return carry

    lax.fori_loop(0, RD // 4, block, 0)


def project_grad(gm, w2, depthed, slope):
    tokens = RD * CD
    ring = tokens + 2 * CD
    return pl.pallas_call(
        project_grad_kernel,
        out_shape=[
            jax.ShapeDtypeStruct((ring, E), bf16),
            jax.ShapeDtypeStruct((E, C), f32),
            jax.ShapeDtypeStruct((tokens, C), bf16),
        ],
        scratch_shapes=[pltpu.VMEM((CD * 40, C), f32)],
        compiler_params=pltpu.CompilerParams(vmem_limit_bytes=VMEM_LIMIT),
        cost_estimate=pl.CostEstimate(
            flops=4 * tokens * C * E, bytes_accessed=tokens * (6 * E + 4 * C), transcendentals=0
        ),
        name="project_grad",
    )(gm, w2, depthed, slope)


def depth_grad_kernel(
    b_ref,
    strip_ref,
    ss_ref,
    w2_ref,
    dw_ref,
    e_ref,
    s_ref,
    n_ref,
    gp_ref,
    gq_ref,
    go_ref,
    gb_ref,
    x_ref,
    pack_ref,
    ext,
    sums,
    total,
):
    w2 = w2_ref[...].astype(bf16)
    strip = strip_ref[...].reshape(2 * 48, C)
    for g in range(GROUPS):
        wide = dot(strip, w2[lane_group(g)], NT).reshape(2, 48, LANES)
        wide = (wide * ss_ref[:, :, lane_group(g)].astype(f32)).astype(bf16).astype(f32)
        for row in range(RD + 2):
            ext[g, row, 15:16, :] = wide[0, row : row + 1]
            ext[g, row, 16 + CD : 17 + CD, :] = wide[1, row : row + 1]

    def fill(first, count):
        for k in range(count):
            for g in range(GROUPS):
                part = b_ref[first + k, :, lane_group(g)]
                ext[g, first + k, 16 : 16 + CD, :] = part.astype(f32)

    fill(0, 2)
    sums[...] = jnp.zeros(sums.shape, f32)
    total[...] = jnp.zeros(total.shape, f32)

    def add_grad(i, weight=1.0):
        four = pl.ds(pl.multiple_of(i * 4 * CD, 4 * CD), 4 * CD)
        wide = dot(n_ref[four, :], x_ref[four, :], TN) * weight
        for g in range(GROUPS):
            total[lane_group(g), :] += wide[:, lane_group(g)]

    x_ref[0 : 4 * CD, :] = jnp.zeros((4 * CD, E), bf16)

    def block(i, carry):
        fill(i * 4 + 2, 4)
        add_grad(jnp.maximum(i - 1, 0), jnp.where(i > 0, 1.0, 0.0))
        for k in range(4):
            row = i * 4 + k
            at = pl.ds(pl.multiple_of(row * CD, CD), CD)
            for g in range(GROUPS):
                held = [sums[g, t] for t in range(9)]
                for q in range(0, CD, 16):
                    here = pl.ds(pl.multiple_of(row * CD + q, 16), 16)
                    own = e_ref[here, lane_group(g)].astype(f32)
                    running = None
                    for t in range(9):
                        left = 15 + t % 3 + q
                        window = ext[g, row + t // 3, left : left + 16, :]
                        term = dw_ref[8 - t : 9 - t, lane_group(g)] * window
                        running = term if running is None else running + term
                        part = own * window
                        held[8 - t] = held[8 - t] + (part[0:8] + part[8:16])
                    wide = running * s_ref[here, lane_group(g)].astype(f32)
                    x_ref[here, lane_group(g)] = wide.astype(bf16)
                for t in range(9):
                    sums[g, t] = held[t]
        return carry

    lax.fori_loop(0, RD // 4, block, 0)
    add_grad(RD // 4 - 1)
    pack_ref[ROW_EXPAND : ROW_EXPAND + E, :] = total[...].astype(bf16)
    pack_ref[ROW_PROJECT : ROW_PROJECT + E, :] = gp_ref[...].astype(bf16)
    pack_ref[ROW_QKV : ROW_QKV + 3 * C, :] = gq_ref[...].astype(bf16)
    pack_ref[ROW_OUT : ROW_OUT + C, :] = go_ref[...].astype(bf16)
    for g in range(GROUPS):
        kernel_sums = jnp.sum(sums[g], axis=1)
        kernel_sums = jnp.concatenate([kernel_sums, jnp.zeros((7, LANES), f32)], axis=0)
        pack_ref[ROW_KERNEL + 16 * g : ROW_KERNEL + 16 * g + 16, :] = kernel_sums.astype(bf16)
    table = jnp.concatenate([gb_ref[:, :LANES], gb_ref[:, LANES:]], axis=0)
    pack_ref[ROW_BIAS : ROW_BIAS + 16, :] = table.astype(bf16)
    pack_ref[ROWS_USED:PACK_ROWS, :] = jnp.zeros((PACK_ROWS - ROWS_USED, C), bf16)


def depth_grad(before, strip, ss, w2, taps, expanded, slope, normed, gp, gq, go, gb):
    tokens = RD * CD
    return pl.pallas_call(
        depth_grad_kernel,
        out_shape=[
            jax.ShapeDtypeStruct((tokens, E), bf16),
            jax.ShapeDtypeStruct((PACK_ROWS, C), bf16),
        ],
        scratch_shapes=[
            pltpu.VMEM((GROUPS, RD + 2, 96, LANES), f32),
            pltpu.VMEM((GROUPS, 9, 8, LANES), f32),
            pltpu.VMEM((E, C), f32),
        ],
        compiler_params=pltpu.CompilerParams(vmem_limit_bytes=VMEM_LIMIT),
        cost_estimate=pl.CostEstimate(
            flops=2 * tokens * C * E + 60 * tokens * E,
            bytes_accessed=tokens * (8 * E + 4 * C),
            transcendentals=0,
        ),
        name="depth_grad",
    )(
        before.reshape(RD + 2, CD, E), strip, ss, w2, taps, expanded, slope, normed, gp, gq, go, gb
    )


def image_grad_kernel(g_ref, w_ref, gain_ref, x_ref, m_ref, o_ref):
    w = w_ref[...].astype(bf16)

    def step(i, carry):
        at = pl.ds(pl.multiple_of(i * 256, 256), 256)
        scaled = dot(g_ref[at, :], w, NT) * gain_ref[...]
        inverse, unit = normalise(x_ref[at, :].astype(f32))
        mean = jnp.mean(scaled * unit, axis=-1, keepdims=True)
        o_ref[at, :] = (m_ref[at, :].astype(f32) + inverse * (scaled - unit * mean)).astype(bf16)
        return carry

    lax.fori_loop(0, x_ref.shape[0] // 256, step, 0)


def image_grad(g, w, gain, x, gm):
    tokens = x.shape[0]
    return pl.pallas_call(
        image_grad_kernel,
        out_shape=jax.ShapeDtypeStruct((tokens, C), bf16),
        compiler_params=pltpu.CompilerParams(vmem_limit_bytes=VMEM_LIMIT),
        cost_estimate=pl.CostEstimate(
            flops=2 * tokens * C * E, bytes_accessed=tokens * (2 * E + 6 * C), transcendentals=0
        ),
        name="image_grad",
    )(g, w, gain, x, gm)


def sum_parts_kernel(factor, x_hbm, o_hbm, x_ref, o_ref, xs, outs):
    x_in = Blocks(x_hbm, x_ref, xs, 32)
    x_in.start_all()
    total = jnp.zeros(x_ref.shape[1:], f32)
    for i in range(4):
        x_in.copy(i).wait()
        for k in range(32):
            total = total + x_ref[32 * i + k].astype(f32)
    total = (total * factor).astype(bf16)
    for k in range(16):
        o_ref[k] = total
    spread = [(o_ref, o_hbm.at[pl.ds(16 * k, 16)]) for k in range(8)]
    spread = copies(spread, outs)
    for copy in spread:
        copy.start()
    for copy in spread:
        copy.wait()


def sum_parts(x, factor):
    return pl.pallas_call(
        lambda *refs: sum_parts_kernel(factor, *refs),
        out_shape=jax.ShapeDtypeStruct(x.shape, bf16),
        in_specs=[HBM],
        out_specs=HBM,
        scratch_shapes=[
            pltpu.VMEM(x.shape, bf16),
            pltpu.VMEM((16,) + x.shape[1:], bf16),
            pltpu.SemaphoreType.DMA((4,)),
            pltpu.SemaphoreType.DMA((8,)),
        ],
        compiler_params=pltpu.CompilerParams(vmem_limit_bytes=VMEM_LIMIT),
        cost_estimate=pl.CostEstimate(
            flops=2 * x.size, bytes_accessed=4 * x.size, transcendentals=0
        ),
        name="sum_parts",
    )(x)


def column_sums(x):
    line = jnp.sum(x, axis=1, keepdims=True)
    return jnp.broadcast_to(line, (C, C)).T[0:1]


def unpack_kernel(
    p_ref, w1_ref, wq_ref, gain1_ref, gain2_ref, g1_ref, ex_ref, k_ref, pr_ref, g2_ref, qk_ref,
    o_ref, b_ref
):
    first = jnp.zeros((C, C), f32)
    second = jnp.zeros((C, C), f32)
    for g in range(GROUPS):
        part = p_ref[ROW_EXPAND + g * C : ROW_EXPAND + (g + 1) * C, :].astype(f32)
        ex_ref[:, lane_group(g)] = part
        first = first + part * w1_ref[:, lane_group(g)].astype(bf16).astype(f32)
        part = p_ref[ROW_PROJECT + g * C : ROW_PROJECT + (g + 1) * C, :].astype(f32)
        pr_ref[g * C : (g + 1) * C, :] = part.T
        part = p_ref[ROW_KERNEL + g * 16 : ROW_KERNEL + (g + 1) * 16, :].astype(f32)
        k_ref[:, lane_group(g)] = part[0:9]
    for k in range(3):
        part = p_ref[ROW_QKV + k * C : ROW_QKV + (k + 1) * C, :].astype(f32)
        qk_ref[:, lane_group(k)] = part
        second = second + part * wq_ref[:, lane_group(k)].astype(bf16).astype(f32)
    g1_ref[...] = column_sums(first) / gain1_ref[...]
    g2_ref[...] = column_sums(second) / gain2_ref[...]
    o_ref[...] = p_ref[ROW_OUT : ROW_OUT + C, :].astype(f32)
    part = p_ref[ROW_BIAS : ROW_BIAS + 16, :].astype(f32)
    table = jnp.concatenate([part[0:4], part[8:12]], axis=1)
    b_ref[...] = jnp.concatenate([table[:, 16 * k : 16 * k + 15] for k in range(15)], axis=1)


def unpack(pack, w1, wq, gain1, gain2):
    return pl.pallas_call(
        unpack_kernel,
        out_shape=[
            jax.ShapeDtypeStruct((1, C), f32),
            jax.ShapeDtypeStruct((C, E), f32),
            jax.ShapeDtypeStruct((9, E), f32),
            jax.ShapeDtypeStruct((E, C), f32),
            jax.ShapeDtypeStruct((1, C), f32),
            jax.ShapeDtypeStruct((C, 3 * C), f32),
            jax.ShapeDtypeStruct((C, C), f32),
            jax.ShapeDtypeStruct((HEADS, 225), f32),
        ],
        compiler_params=pltpu.CompilerParams(vmem_limit_bytes=VMEM_LIMIT),
        cost_estimate=pl.CostEstimate(
            flops=4 * pack.size, bytes_accessed=6 * pack.size, transcendentals=0
        ),
        name="unpack",
    )(pack, w1, wq, gain1, gain2)


def swap_ends(low, high, axis, beside=None):
    count = lax.axis_size(axis)
    odd = lax.axis_index(axis) % 2 == 1
    pairs = [(i, i ^ 1) for i in range(count)]
    others = [(i, ((i - 1) ^ 1) + 1) for i in range(1, count - 1)]
    first = lax.ppermute(jnp.where(odd, low, high), axis, pairs)
    second = lax.ppermute(jnp.where(odd, high, low), axis, others)
    if beside is not None:
        first, beside = lax.optimization_barrier((first, beside))
    ends = jnp.where(odd, first, second), jnp.where(odd, second, first)
    return ends if beside is None else (ends, beside)


def per_device(
    image,
    cotangent,
    norm1_gain,
    w_expand,
    dw_kernel,
    w_project,
    norm2_gain,
    w_qkv,
    w_out,
    bias_table,
):
    factor = 1.0 / math.sqrt(RD * CD * 128)
    w1, w2, wq, wo = w_expand, w_project, w_qkv, w_out
    gain1 = norm1_gain.reshape(1, C)
    gain2 = norm2_gain.reshape(1, C)
    tokens = image.reshape(RD * CD, C)
    above, below = swap_ends(tokens[: 2 * CD], tokens[(RD - 2) * CD :], "rows")
    above = above.reshape(2, CD, C)
    below = below.reshape(2, CD, C)
    left = jnp.concatenate([above[:, :2], image[:, :2], below[:, :2]], axis=0)
    right = jnp.concatenate([above[:, -2:], image[:, -2:], below[:, -2:]], axis=0)
    left = left.transpose(1, 0, 2)
    right = right.transpose(1, 0, 2)
    (before_left, after_right), late_gain = swap_ends(left, right, COLS, gain1)
    expanded, slope1, normed1 = expand(tokens, late_gain, w1)
    halo = jnp.concatenate([above, below], axis=0)
    strip = jnp.concatenate([before_left, left[:1], right[1:], after_right], axis=0)
    strip = jnp.pad(strip, ((0, 0), (0, 12), (0, 0)))
    send, depthed, slope2, slope2_strip = depth(
        expanded, tokens, to_columns(cotangent), halo, strip, gain1, w1, dw_kernel, w2
    )
    windows = lax.all_to_all(send, PLANE, 0, 0, tiled=True)
    back, grad_qkv, grad_out, grad_bias = attend(windows, gain2, wq, wo, bias_table)
    back = lax.all_to_all(back, PLANE, 0, 0, tiled=True)
    grad_left, grad_right = swap_ends(back[0, :40], back[31, 40:80], COLS)
    before, grad_project, grad_middle = project_grad(back, w2, depthed, slope2)
    grad_strip = jnp.pad(jnp.stack([grad_left, grad_right]), ((0, 0), (0, 8), (0, 0)))
    grad_wide, pack = depth_grad(
        before, grad_strip, slope2_strip, w2, dw_kernel, expanded, slope1, normed1,
        grad_project, grad_qkv, grad_out, grad_bias,
    )
    parts = lax.all_to_all(pack.reshape(128, 16, C), ALL, 0, 0, tiled=True)
    grad_wide, parts = lax.optimization_barrier((grad_wide, parts))
    grad_image = image_grad(grad_wide, w1, gain1, tokens, grad_middle)
    block_out = from_columns(back)
    whole = lax.all_to_all(sum_parts(parts, factor), ALL, 0, 0, tiled=True)
    g1, ge, gk, gp, g2, gq, go, gb = unpack(whole.reshape(PACK_ROWS, C), w1, wq, gain1, gain2)
    return (
        block_out,
        grad_image.reshape(RD, CD, C),
        g1.reshape(C),
        ge,
        gk,
        gp,
        g2.reshape(C),
        gq,
        go,
        gb,
    )


def solution(mesh):
    mesh = Mesh(mesh.devices.reshape(4, 8, 4), ALL)
    tiles = P("rows", COLS, None)
    return jax.shard_map(
        per_device,
        mesh=mesh,
        in_specs=(tiles, tiles) + (P(),) * 8,
        out_specs=(tiles, tiles) + (P(),) * 8,
        check_vma=False,
    )
```
